32 devices in a mesh: groups: 2 (over y), hid: 4 (over z), dp: 2 (over x), col: 2 (over core).
Axes of the slice: x: 2, y: 2, z: 4, core: 2. Of those that a mesh axis runs over, the one named last changes fastest.
Arguments:
- tokens: bfloat16 [512, 4096], P(('groups', 'hid', 'dp'), 'col'), parts along dimension 0, may hold values from -6 to 6
- target: bfloat16 [512, 4096], P(('groups', 'hid', 'dp'), 'col'), parts along dimension 0, may hold values from -6 to 6
- gate_panel: bfloat16 [8, 2, 64, 40960], P(('groups', 'hid'), 'col'), parts along dimension 0, may hold values from -0.1875 to 0.1875
- up_panel: bfloat16 [8, 2, 64, 40960], P(('groups', 'hid'), 'col'), parts along dimension 0, may hold values from -0.1875 to 0.1875
- down_panel: bfloat16 [8, 2, 64, 40960], P(('groups', 'hid'), 'col'), parts along dimension 0, may hold values from -0.09375 to 0.09375
- gate_list: int32 [8, 2, 640], P(('groups', 'hid'), 'col'), parts along dimension 0, may hold values from 0 to 2048, as said below
- up_list: int32 [8, 2, 640], P(('groups', 'hid'), 'col'), parts along dimension 0, may hold values from 0 to 2048, as said below
- down_list: int32 [8, 2, 640], P(('groups', 'hid'), 'col'), parts along dimension 0, may hold values from 0 to 2048, as said below
Outputs:
- gate_grad: bfloat16 [8, 2, 64, 40960], P(('groups', 'hid'), 'col', None, 'dp'), parts along dimension 0
- up_grad: bfloat16 [8, 2, 64, 40960], P(('groups', 'hid'), 'col', None, 'dp'), parts along dimension 0
- down_grad: bfloat16 [8, 2, 64, 40960], P(('groups', 'hid'), 'col', None, 'dp'), parts along dimension 0
The draws below stay inside these ranges and needn't reach their ends.
There are 2 independent parts, one for each index of `groups`. The reference program is written for one: setup_inputs(seed, part) draws one part's arguments, and reference() takes and returns one part's arrays. A program takes and returns all parts, laid end to end along the dimension named above; each array names one. Nothing has to cross between parts.
Inputs may be any that keep to these rules, and one draw needn't show every extreme that they name: `gate_list`: in each list[h, c] the entries below 2048 are distinct and fill the first slots; the rest equal 2048. Each list[h, c] has between 384 and 640 entries below 2048, and some list[h, c] has exactly 640. `up_list`: as for gate_list. `down_list`: as for gate_list.
All inputs are finite; a program needn't handle non-finite values.
Results may differ from the reference program's by a relative error of at most 0.0069.
Values may be sent and summed in bfloat16 or wider, within the bound.
No kernel may reach another device: no remote copies, remote signals or barrier semaphores. Data moves between devices by JAX's collectives and lax.ppermute only.
A program may use at most 384 MiB of HBM per device.

```python
import jax
import jax.numpy as jnp
from jax import lax

D = 4096
FF = 16384
BLK = 64
TOK_DEV = 128
TOKENS = 256
SLAB_BLK = 64
ROW_BLK = 32
GRID = 2048
CAP = 640
N_HID = 4
N_DP = 2
N_COL = 2


def block_lists(key):
    key_counts, key_fullest, key_scores = jax.random.split(key, 3)
    devices = N_HID * N_COL
    lowest = GRID * 3 // 16
    counts = jax.random.randint(key_counts, (devices,), lowest, CAP + 1, dtype=jnp.int32)
    fullest = jax.random.randint(key_fullest, (), 0, devices, dtype=jnp.int32)
    counts = jnp.where(jnp.arange(devices, dtype=jnp.int32) == fullest, CAP, counts)
    spread = max(1, 2 ** 30 // GRID)
    scores = jax.random.randint(key_scores, (devices, GRID), 0, spread, dtype=jnp.int32) * GRID + jnp.arange(GRID, dtype=jnp.int32)[None, :]
    ordering = jnp.argsort(scores, axis=1)[:, :CAP].astype(jnp.int32)
    listed = jnp.where(jnp.arange(CAP, dtype=jnp.int32)[None, :] < counts[:, None], ordering, GRID)
    return listed.reshape(N_HID, N_COL, CAP).astype(jnp.int32)


def draw_gate_list(key, part):
    key = jax.random.fold_in(key, 11)
    return block_lists(key)


def draw_up_list(key, part):
    key = jax.random.fold_in(key, 23)
    return block_lists(key)


def draw_down_list(key, part):
    key = jax.random.fold_in(key, 37)
    return block_lists(key)


def steps_of(rng, extent, cuts, smallest, high):
    loudness, own = 1.0, jax.random.fold_in(rng, 6)
    for dim, blocks in cuts:
        steps = jnp.exp(jax.random.uniform(jax.random.fold_in(own, dim), (blocks,), jnp.float32, smallest / len(cuts), high / len(cuts)))
        loudness = loudness * jnp.repeat(steps, extent[dim] // blocks).reshape([-1 if axis == dim else 1 for axis in range(len(extent))])
    return loudness


def gaussian(own_key, dims, width, most, pieces=(), kind=jnp.bfloat16):
    entries = width * jax.random.normal(own_key, dims, jnp.float32)
    if pieces:
        entries = entries * steps_of(own_key, dims, pieces, -0.22, 0.18)
    return jnp.clip(entries, -most, most).astype(kind)


def setup_inputs(seed: int = 0, part: int = 0) -> dict:
    key_list = jax.random.split(jax.random.key(seed), 9)
    part_splits = jax.random.split(jax.random.fold_in(key_list[8], part), 9)
    return {
        "tokens": gaussian(part_splits[0], (TOKENS, D), 1.0, 6.0, ((0, 8), (1, 2))),
        "target": gaussian(part_splits[1], (TOKENS, D), 1.0, 6.0, ((0, 8), (1, 2))),
        "gate_panel": gaussian(part_splits[2], (N_HID, N_COL, BLK, CAP * BLK), (D // 4) ** -0.5, 0.1875, ((0, 4), (1, 2))),
        "up_panel": gaussian(part_splits[3], (N_HID, N_COL, BLK, CAP * BLK), (D // 4) ** -0.5, 0.1875, ((0, 4), (1, 2))),
        "down_panel": gaussian(part_splits[4], (N_HID, N_COL, BLK, CAP * BLK), (FF // 4) ** -0.5, 0.09375, ((0, 4), (1, 2))),
        "gate_list": draw_gate_list(jax.random.fold_in(jax.random.fold_in(key_list[8], part), 71), part),
        "up_list": draw_up_list(jax.random.fold_in(jax.random.fold_in(key_list[8], part), 71), part),
        "down_list": draw_down_list(jax.random.fold_in(jax.random.fold_in(key_list[8], part), 71), part),
    }


SLOPE_SCALE = 0.0625
HIGHEST = lax.Precision.HIGHEST


def assemble(slot_panel, block_list, rows_are_hidden):
    blocks = slot_panel.astype(jnp.float32).reshape(N_HID, N_COL, BLK, CAP, BLK)
    blocks = blocks.transpose(0, 1, 3, 2, 4).reshape(N_HID, N_COL, CAP, BLK * BLK)
    onehot = (jnp.arange(GRID, dtype=jnp.int32)[None, None, :, None] == block_list.astype(jnp.int32)[:, :, None, :]).astype(jnp.float32)
    placed = jnp.einsum("hcgs,hcsk->hcgk", onehot, blocks, precision=HIGHEST)
    placed = placed.reshape(N_HID, N_COL, ROW_BLK, SLAB_BLK, BLK, BLK)
    if rows_are_hidden:
        return placed.transpose(0, 3, 4, 1, 2, 5).reshape(FF, D)
    return placed.transpose(1, 2, 4, 0, 3, 5).reshape(D, FF)


def collect(grad_matrix, block_list, rows_are_hidden):
    if rows_are_hidden:
        tile_rows = grad_matrix.reshape(N_HID, SLAB_BLK, BLK, N_COL, ROW_BLK, BLK).transpose(0, 3, 4, 1, 2, 5)
    else:
        tile_rows = grad_matrix.reshape(N_COL, ROW_BLK, BLK, N_HID, SLAB_BLK, BLK).transpose(3, 0, 1, 4, 2, 5)
    tile_rows = tile_rows.reshape(N_HID, N_COL, GRID, BLK * BLK)
    tile_rows = jnp.concatenate([tile_rows, jnp.zeros((N_HID, N_COL, 1, BLK * BLK), tile_rows.dtype)], axis=2)
    where_rows = jnp.broadcast_to(block_list.astype(jnp.int32)[:, :, :, None], (N_HID, N_COL, CAP, BLK * BLK))
    picked = jnp.take_along_axis(tile_rows, where_rows, axis=2)
    picked = picked.reshape(N_HID, N_COL, CAP, BLK, BLK).transpose(0, 1, 3, 2, 4)
    return picked.reshape(N_HID, N_COL, BLK, CAP * BLK)


def per_replica(values):
    row_width = values.shape[1]
    grouped = values.reshape(N_HID, N_DP, TOK_DEV // N_HID, row_width).transpose(1, 0, 2, 3)
    return grouped.reshape(N_DP, TOK_DEV, row_width)


def reference(tokens, target, gate_panel, up_panel, down_panel, gate_list, up_list, down_list):
    gate_matrix = assemble(gate_panel, gate_list, False)
    up_matrix = assemble(up_panel, up_list, False)
    down_matrix = assemble(down_panel, down_list, True)
    inputs = tokens.astype(jnp.float32)
    gate = jnp.dot(inputs, gate_matrix, precision=HIGHEST)
    up = jnp.dot(inputs, up_matrix, precision=HIGHEST)
    sigmoid_gate = jax.nn.sigmoid(gate)
    silu_gate = gate * sigmoid_gate
    hidden = (silu_gate * up).astype(jnp.bfloat16)
    output = jnp.dot(hidden.astype(jnp.float32), down_matrix, precision=HIGHEST)
    slope = ((output - target.astype(jnp.float32)) * SLOPE_SCALE).astype(jnp.bfloat16)
    back = jnp.dot(slope.astype(jnp.float32), down_matrix.T, precision=HIGHEST)
    gate_slope = (back * up * sigmoid_gate * (1.0 + gate * (1.0 - sigmoid_gate))).astype(jnp.bfloat16)
    up_slope = (back * silu_gate).astype(jnp.bfloat16)
    inputs_r = per_replica(inputs)
    gate_slope_r = per_replica(gate_slope.astype(jnp.float32))
    up_slope_r = per_replica(up_slope.astype(jnp.float32))
    hidden_r = per_replica(hidden.astype(jnp.float32))
    slope_r = per_replica(slope.astype(jnp.float32))
    gate_total = jnp.zeros((D, FF), jnp.float32)
    up_total = jnp.zeros((D, FF), jnp.float32)
    down_total = jnp.zeros((FF, D), jnp.float32)
    for replica in range(N_DP):
        gate_total = gate_total + jnp.dot(inputs_r[replica].T, gate_slope_r[replica], precision=HIGHEST).astype(jnp.bfloat16).astype(jnp.float32)
        up_total = up_total + jnp.dot(inputs_r[replica].T, up_slope_r[replica], precision=HIGHEST).astype(jnp.bfloat16).astype(jnp.float32)
        down_total = down_total + jnp.dot(hidden_r[replica].T, slope_r[replica], precision=HIGHEST).astype(jnp.bfloat16).astype(jnp.float32)
    gate_grad = collect(gate_total, gate_list, False).astype(jnp.bfloat16)
    up_grad = collect(up_total, up_list, False).astype(jnp.bfloat16)
    down_grad = collect(down_total, down_list, True).astype(jnp.bfloat16)
    return (gate_grad, up_grad, down_grad)
```

```python
import functools

import jax
import jax.numpy as jnp
from jax import lax
from jax.experimental import pallas as pl
from jax.experimental.pallas import tpu as pltpu
from jax.sharding import PartitionSpec as P

D = 4096
FF = 16384
BLK = 64
PAIR = 2 * BLK
SLOPE_SCALE = 0.0625
VMEM_BYTES = 52 * 2**20


def left_half():
    return lax.broadcasted_iota(jnp.int32, (BLK, PAIR), 1) < BLK


def swap_halves(tile):
    return jnp.concatenate([tile[:, BLK:], tile[:, :BLK]], axis=1)


def densify_kernel(half_cap, rows_per_step, n_cols, table, panel, out, tiles):
    step = pl.program_id(0)

    @pl.when(step == 0)
    def _():
        tiles[2 * half_cap] = jnp.zeros((BLK, PAIR), tiles.dtype)

        def stage(t, carry):
            tile = panel[:, pl.ds(pl.multiple_of(t * PAIR, PAIR), PAIR)]
            tiles[t] = tile
            tiles[half_cap + t] = swap_halves(tile)
            return carry

        lax.fori_loop(0, half_cap, stage, 0, unroll=4)

    mask = left_half()

    def row(i, carry):
        base = (step * rows_per_step + i) * n_cols
        for p in range(n_cols // 2):
            left = tiles[table[base + 2 * p]]
            right = tiles[table[base + 2 * p + 1]]
            out[pl.ds(pl.multiple_of(i * BLK, BLK), BLK), p * PAIR : (p + 1) * PAIR] = jnp.where(
                mask, left, right
            )
        return carry

    lax.fori_loop(0, rows_per_step, row, 0)


def densify(panel, table):
    n_rows, n_cols = table.shape
    half_cap = panel.shape[1] // PAIR
    rows_per_step = 4
    return pl.pallas_call(
        functools.partial(densify_kernel, half_cap, rows_per_step, n_cols),
        grid_spec=pltpu.PrefetchScalarGridSpec(
            num_scalar_prefetch=1,
            grid=(n_rows // rows_per_step,),
            in_specs=[pl.BlockSpec(panel.shape, lambda s, *_: (0, 0))],
            out_specs=pl.BlockSpec((rows_per_step * BLK, n_cols * BLK), lambda s, *_: (s, 0)),
            scratch_shapes=[pltpu.VMEM((2 * half_cap + 1, BLK, PAIR), panel.dtype)],
        ),
        out_shape=jax.ShapeDtypeStruct((n_rows * BLK, n_cols * BLK), panel.dtype),
        compiler_params=pltpu.CompilerParams(vmem_limit_bytes=VMEM_BYTES),
        cost_estimate=pl.CostEstimate(
            flops=0, bytes_accessed=2 * panel.size + 2 * n_rows * n_cols * BLK * BLK, transcendentals=0
        ),
        name="densify",
    )(table.reshape(-1), panel)


def gradient_kernel(n_steps, rows_per_step, n_cols, picks, lhs, rhs, out, tiles):
    step = pl.program_id(0)
    col_pairs = n_cols // 2
    width = min(4, col_pairs)
    for c in range(0, col_pairs, width):
        part = jnp.dot(
            lhs[...], rhs[:, c * PAIR : (c + width) * PAIR], preferred_element_type=jnp.float32
        ).astype(tiles.dtype)
        for i in range(rows_per_step):
            for p in range(width):
                tiles[(step * rows_per_step + i) * col_pairs + c + p] = part[
                    i * BLK : (i + 1) * BLK, p * PAIR : (p + 1) * PAIR
                ]

    @pl.when(step == n_steps - 1)
    def _():
        tiles[n_steps * rows_per_step * col_pairs] = jnp.zeros((BLK, PAIR), tiles.dtype)
        mask = left_half()

        def fetch(code):
            tile = tiles[code // 2]
            return jnp.where(code % 2 == 1, swap_halves(tile), tile)

        def pick(k, carry):
            out[:, pl.ds(pl.multiple_of(k * PAIR, PAIR), PAIR)] = jnp.where(
                mask, fetch(picks[2 * k]), fetch(picks[2 * k + 1])
            )
            return carry

        lax.fori_loop(0, out.shape[1] // PAIR, pick, 0, unroll=2)


def gradient(lhs, rhs, picks):
    n_rows, n_cols = lhs.shape[0] // BLK, rhs.shape[1] // BLK
    rows_per_step = 4
    n_steps = n_rows // rows_per_step
    return pl.pallas_call(
        functools.partial(gradient_kernel, n_steps, rows_per_step, n_cols),
        grid_spec=pltpu.PrefetchScalarGridSpec(
            num_scalar_prefetch=1,
            grid=(n_steps,),
            in_specs=[
                pl.BlockSpec((rows_per_step * BLK, lhs.shape[1]), lambda s, *_: (s, 0)),
                pl.BlockSpec(rhs.shape, lambda s, *_: (0, 0)),
            ],
            out_specs=pl.BlockSpec((BLK, picks.shape[0] * BLK), lambda s, *_: (0, 0)),
            scratch_shapes=[pltpu.VMEM((n_rows * n_cols // 2 + 1, BLK, PAIR), jnp.bfloat16)],
        ),
        out_shape=jax.ShapeDtypeStruct((BLK, picks.shape[0] * BLK), jnp.bfloat16),
        compiler_params=pltpu.CompilerParams(vmem_limit_bytes=VMEM_BYTES),
        cost_estimate=pl.CostEstimate(
            flops=2 * lhs.shape[0] * lhs.shape[1] * rhs.shape[1],
            bytes_accessed=2 * (lhs.size + rhs.size + picks.shape[0] * BLK * BLK),
            transcendentals=0,
        ),
        name="gradient",
    )(picks, lhs, rhs)


def tile_table(block_ids, row_blocks, slab_blocks, rows_are_hidden):
    cap = block_ids.shape[0]
    grid = row_blocks * slab_blocks
    slot = jnp.arange(1, cap + 1, dtype=jnp.int32)
    held = jnp.sum(
        jnp.where(block_ids[None, :] == jnp.arange(grid, dtype=jnp.int32)[:, None], slot[None, :], 0), axis=1
    )
    held = held.reshape(row_blocks, slab_blocks)
    if rows_are_hidden:
        held = held.T
    half = jnp.arange(held.shape[1], dtype=jnp.int32)[None, :] % 2
    index = held - 1
    tile = index // 2 + jnp.where(index % 2 != half, cap // 2, 0)
    return jnp.where(held > 0, tile, cap)


def pick_codes(block_ids, row_blocks, slab_blocks, rows_are_hidden):
    grid = row_blocks * slab_blocks
    row, col = block_ids // slab_blocks, block_ids % slab_blocks
    cols = slab_blocks
    if rows_are_hidden:
        row, col, cols = col, row, row_blocks
    half = jnp.arange(block_ids.shape[0], dtype=jnp.int32) % 2
    code = 2 * (row * (cols // 2) + col // 2) + jnp.where(col % 2 != half, 1, 0)
    return jnp.where(block_ids < grid, code, grid)


def shift(values, axis, k):
    n = lax.axis_size(axis)
    return values if k == 0 else lax.ppermute(values, axis, [(i, i ^ k) for i in range(n)])


def gather_rows(values):
    near = [shift(values, "hid", k) for k in range(lax.axis_size("hid"))]
    return [[shift(v, "dp", j) for v in near] for j in range(lax.axis_size("dp"))]


def swap_cores(values):
    return lax.ppermute(values, "col", [(0, 1), (1, 0)])


def f32(values):
    return values.astype(jnp.float32)


def local(tokens, target, gate_panel, up_panel, down_panel, gate_list, up_list, down_list):
    n_hid, n_dp = lax.axis_size("hid"), lax.axis_size("dp")
    slab_blocks = FF // BLK // n_hid
    row_blocks = D // BLK // lax.axis_size("col")
    rows = tokens.shape[0]
    own = rows * n_hid

    shards = gather_rows(tokens)
    inputs = jnp.concatenate([v for part in shards for v in part])

    gate_w = densify(gate_panel[0, 0], tile_table(gate_list[0, 0], row_blocks, slab_blocks, False))
    up_w = densify(up_panel[0, 0], tile_table(up_list[0, 0], row_blocks, slab_blocks, False))
    down_w = densify(down_panel[0, 0], tile_table(down_list[0, 0], row_blocks, slab_blocks, True))

    def mine(block_list):
        share = block_list.shape[-1] // n_dp
        return lax.dynamic_slice_in_dim(block_list[0, 0], lax.axis_index("dp") * share, share)

    gate_codes = pick_codes(mine(gate_list), row_blocks, slab_blocks, False)
    up_codes = pick_codes(mine(up_list), row_blocks, slab_blocks, False)
    down_codes = pick_codes(mine(down_list), row_blocks, slab_blocks, True)

    gate_part = jnp.dot(inputs, gate_w, preferred_element_type=jnp.float32).astype(jnp.bfloat16)
    gate_other = swap_cores(gate_part)
    up_part = jnp.dot(inputs, up_w, preferred_element_type=jnp.float32).astype(jnp.bfloat16)
    up_other = swap_cores(up_part)
    gate = f32(gate_part) + f32(gate_other)
    up = f32(up_part) + f32(up_other)
    sigmoid_gate = jax.nn.sigmoid(gate)
    hidden = (gate * sigmoid_gate * up).astype(jnp.bfloat16)

    out_part = jnp.dot(hidden[:own], down_w, preferred_element_type=jnp.float32).astype(jnp.bfloat16)
    output = f32(out_part[:rows])
    for k in range(1, n_hid):
        output = output + f32(shift(out_part[k * rows : (k + 1) * rows], "hid", k))
    own_slope = ((output - f32(target)) * SLOPE_SCALE).astype(jnp.bfloat16)
    slope_shards = gather_rows(own_slope)
    slope = jnp.concatenate([v for part in slope_shards for v in part])

    back_part = lax.dot_general(
        slope, down_w, (((1,), (1,)), ((), ())), preferred_element_type=jnp.float32
    ).astype(jnp.bfloat16)
    back = f32(back_part) + f32(swap_cores(back_part))
    gate_slope = (back * up * sigmoid_gate * (1.0 + gate * (1.0 - sigmoid_gate))).astype(jnp.bfloat16)
    up_slope = (back * (gate * sigmoid_gate)).astype(jnp.bfloat16)

    inputs_t = inputs.T
    down_grad = gradient(hidden.T, slope, down_codes)
    gate_grad = gradient(inputs_t, gate_slope, gate_codes)
    up_grad = gradient(inputs_t, up_slope, up_codes)
    return gate_grad[None, None], up_grad[None, None], down_grad[None, None]


def solution(mesh):
    return jax.shard_map(
        local,
        mesh=mesh,
        in_specs=(
            P(("groups", "hid", "dp"), "col"),
            P(("groups", "hid", "dp"), "col"),
            P(("groups", "hid"), "col", None, None),
            P(("groups", "hid"), "col", None, None),
            P(("groups", "hid"), "col", None, None),
            P(("groups", "hid"), "col", None),
            P(("groups", "hid"), "col", None),
            P(("groups", "hid"), "col", None),
        ),
        out_specs=(
            P(("groups", "hid"), "col", None, "dp"),
            P(("groups", "hid"), "col", None, "dp"),
            P(("groups", "hid"), "col", None, "dp"),
        ),
        check_vma=False,
    )
```

```python
import functools

import jax
import jax.numpy as jnp
from jax import lax
from jax.experimental import pallas as pl
from jax.experimental.pallas import tpu as pltpu
from jax.sharding import PartitionSpec as P

D = 4096
FF = 16384
BLK = 64
PAIR = 2 * BLK
SLOPE_SCALE = 0.0625
DENSIFY_VMEM = 20 * 2**20
GRADIENT_VMEM = 44 * 2**20


def swap_halves(tile):
    return jnp.concatenate([tile[:, BLK:], tile[:, :BLK]], axis=1)


def join(left, right):
    return jnp.concatenate([left[:, :BLK], right[:, BLK:]], axis=1)


def lanes(t):
    return pl.ds(pl.multiple_of(t * PAIR, PAIR), PAIR)


def largest(options, total):
    return max(n for n in options if total % n == 0)


def densify_kernel(half_cap, rows_per_step, n_cols, chunks, table, panel, out, tiles, sems):
    step = pl.program_id(0)
    share = half_cap // chunks

    @pl.when(step == 0)
    def _():
        copies = []
        for c in range(chunks):
            span = pl.ds(c * share * PAIR, share * PAIR)
            copies.append(pltpu.make_async_copy(panel.at[:, span], tiles.at[:, span], sems.at[c]))
            copies[c].start()
        tiles[:, 2 * half_cap * PAIR :] = jnp.zeros((BLK, PAIR), tiles.dtype)
        batch = largest((1, 2, 4, 5, 8), share)
        for c in range(chunks):
            copies[c].wait()

            def stage(b, carry):
                t = c * share + b * batch
                swapped = [swap_halves(tiles[:, lanes(t + u)]) for u in range(batch)]
                for u in range(batch):
                    tiles[:, lanes(half_cap + t + u)] = swapped[u]
                return carry

            lax.fori_loop(0, share // batch, stage, 0)

    def row(i, carry):
        base = (step * rows_per_step + i) * n_cols
        for p in range(n_cols // 2):
            out[pl.ds(pl.multiple_of(i * BLK, BLK), BLK), p * PAIR : (p + 1) * PAIR] = join(
                tiles[:, lanes(table[base + 2 * p])], tiles[:, lanes(table[base + 2 * p + 1])]
            )
        return carry

    lax.fori_loop(0, rows_per_step, row, 0)


def densify(panel, table):
    n_rows, n_cols = table.shape
    half_cap = panel.shape[1] // PAIR
    rows_per_step = 4
    chunks = largest((1, 2, 4), half_cap)
    return pl.pallas_call(
        functools.partial(densify_kernel, half_cap, rows_per_step, n_cols, chunks),
        grid_spec=pltpu.PrefetchScalarGridSpec(
            num_scalar_prefetch=1,
            grid=(n_rows // rows_per_step,),
            in_specs=[pl.BlockSpec(memory_space=pl.ANY)],
            out_specs=pl.BlockSpec((rows_per_step * BLK, n_cols * BLK), lambda s, *_: (s, 0)),
            scratch_shapes=[
                pltpu.VMEM((BLK, (2 * half_cap + 1) * PAIR), panel.dtype),
                pltpu.SemaphoreType.DMA((chunks,)),
            ],
        ),
        out_shape=jax.ShapeDtypeStruct((n_rows * BLK, n_cols * BLK), panel.dtype),
        compiler_params=pltpu.CompilerParams(vmem_limit_bytes=DENSIFY_VMEM),
        cost_estimate=pl.CostEstimate(
            flops=0, bytes_accessed=4 * panel.size + 4 * n_rows * n_cols * BLK * BLK, transcendentals=0
        ),
        name="densify",
    )(table.reshape(-1), panel)


def gradient_kernel(n_steps, rows_per_step, n_cols, n_rhs, picks, lhs, *refs):
    terms, (out, tiles, rows) = refs[:n_rhs], refs[n_rhs : n_rhs + 3]
    step = pl.program_id(0)
    col_pairs = n_cols // 2
    width = 2
    rhs = terms[0]
    if n_rhs == 3:
        rhs = refs[n_rhs + 3]

        @pl.when(step == 0)
        def _():
            mine, theirs, factor = terms

            def scale(j, carry):
                span = pl.ds(pl.multiple_of(j * 2 * PAIR, 2 * PAIR), 2 * PAIR)
                rhs[:, span] = ((f32(mine[:, span]) + f32(theirs[:, span])) * factor[:, span]).astype(rhs.dtype)
                return carry

            lax.fori_loop(0, col_pairs // 2, scale, 0)

    rows[...] = lhs[...].T
    for c in range(0, col_pairs, width):
        part = jnp.dot(
            rows[...], rhs[:, c * PAIR : (c + width) * PAIR], preferred_element_type=jnp.float32
        ).astype(tiles.dtype)
        for i in range(rows_per_step):
            for p in range(width):
                tiles[(step * rows_per_step + i) * col_pairs + c + p] = part[
                    i * BLK : (i + 1) * BLK, p * PAIR : (p + 1) * PAIR
                ]

    @pl.when(step == n_steps - 1)
    def _():
        tiles[n_steps * rows_per_step * col_pairs] = jnp.zeros((BLK, PAIR), tiles.dtype)

        def fetch(code):
            tile = tiles[code // 2]
            return jnp.where(code % 2 == 1, swap_halves(tile), tile)

        def pick(k, carry):
            out[:, lanes(k)] = join(fetch(picks[2 * k]), fetch(picks[2 * k + 1]))
            return carry

        pairs = out.shape[1] // PAIR
        lax.fori_loop(0, pairs, pick, 0, unroll=largest((1, 2, 5, 8), pairs))


def gradient(lhs, terms, picks):
    n_rows, n_cols = lhs.shape[1] // BLK, terms[0].shape[1] // BLK
    rows_per_step = min(16, n_rows)
    n_steps = n_rows // rows_per_step
    scratch = [
        pltpu.VMEM((n_rows * n_cols // 2 + 1, BLK, PAIR), jnp.bfloat16),
        pltpu.VMEM((rows_per_step * BLK, lhs.shape[0]), jnp.bfloat16),
    ]
    if len(terms) == 3:
        scratch.append(pltpu.VMEM(terms[0].shape, jnp.bfloat16))
    return pl.pallas_call(
        functools.partial(gradient_kernel, n_steps, rows_per_step, n_cols, len(terms)),
        grid_spec=pltpu.PrefetchScalarGridSpec(
            num_scalar_prefetch=1,
            grid=(n_steps,),
            in_specs=[pl.BlockSpec((lhs.shape[0], rows_per_step * BLK), lambda s, *_: (0, s))]
            + [pl.BlockSpec(t.shape, lambda s, *_: (0, 0)) for t in terms],
            out_specs=pl.BlockSpec((BLK, picks.shape[0] * BLK), lambda s, *_: (0, 0)),
            scratch_shapes=scratch,
        ),
        out_shape=jax.ShapeDtypeStruct((BLK, picks.shape[0] * BLK), jnp.bfloat16),
        compiler_params=pltpu.CompilerParams(vmem_limit_bytes=GRADIENT_VMEM),
        cost_estimate=pl.CostEstimate(
            flops=2 * lhs.size * terms[0].shape[1],
            bytes_accessed=2 * lhs.size + 4 * len(terms) * terms[0].size + 2 * picks.shape[0] * BLK * BLK,
            transcendentals=0,
        ),
        name="gradient",
    )(picks, lhs, *terms)


def tile_table(block_ids, row_blocks, slab_blocks, rows_are_hidden):
    cap = block_ids.shape[0]
    grid = row_blocks * slab_blocks
    slot = jnp.arange(1, cap + 1, dtype=jnp.int32)
    held = jnp.sum(
        jnp.where(block_ids[None, :] == jnp.arange(grid, dtype=jnp.int32)[:, None], slot[None, :], 0), axis=1
    )
    held = held.reshape(row_blocks, slab_blocks)
    if rows_are_hidden:
        held = held.T
    half = jnp.arange(held.shape[1], dtype=jnp.int32)[None, :] % 2
    index = held - 1
    tile = index // 2 + jnp.where(index % 2 != half, cap // 2, 0)
    return jnp.where(held > 0, tile, cap)


def pick_codes(block_ids, row_blocks, slab_blocks, rows_are_hidden):
    grid = row_blocks * slab_blocks
    row, col = block_ids // slab_blocks, block_ids % slab_blocks
    cols = slab_blocks
    if rows_are_hidden:
        row, col, cols = col, row, row_blocks
    half = jnp.arange(block_ids.shape[0], dtype=jnp.int32) % 2
    code = 2 * (row * (cols // 2) + col // 2) + jnp.where(col % 2 != half, 1, 0)
    return jnp.where(block_ids < grid, code, grid)


def shift(values, axis, k):
    n = lax.axis_size(axis)
    return values if k == 0 else lax.ppermute(values, axis, [(i, i ^ k) for i in range(n)])


def gather_near(values):
    return [shift(values, "hid", k) for k in range(lax.axis_size("hid"))]


def gather_far(near):
    far = [shift(v, "dp", j) for j in range(1, lax.axis_size("dp")) for v in near]
    return near + far


def swap_cores(values):
    return lax.ppermute(values, "col", [(0, 1), (1, 0)])


def f32(values):
    return values.astype(jnp.float32)


def whole(mine, theirs):
    return f32(mine) + f32(theirs)


def activation(gate, up):
    return (gate * jax.nn.sigmoid(gate) * up).astype(jnp.bfloat16)


def local(tokens, target, gate_panel, up_panel, down_panel, gate_list, up_list, down_list):
    n_hid, n_dp = lax.axis_size("hid"), lax.axis_size("dp")
    slab_blocks = FF // BLK // n_hid
    row_blocks = D // BLK // lax.axis_size("col")
    rows = tokens.shape[0]
    own = rows * n_hid

    gate_table = tile_table(gate_list[0, 0], row_blocks, slab_blocks, False)
    up_table = tile_table(up_list[0, 0], row_blocks, slab_blocks, False)
    down_table = tile_table(down_list[0, 0], row_blocks, slab_blocks, True)

    near = gather_near(tokens)
    gate_w = densify(gate_panel[0, 0], gate_table)
    near, gate_w = lax.optimization_barrier((near, gate_w))
    shards = gather_far(near)
    up_w = densify(up_panel[0, 0], up_table)
    shards, up_w = lax.optimization_barrier((shards, up_w))
    inputs = jnp.concatenate(shards)

    def mine(block_list):
        share = block_list.shape[-1] // n_dp
        return lax.dynamic_slice_in_dim(block_list[0, 0], lax.axis_index("dp") * share, share)

    gate_part = jnp.dot(inputs, gate_w, preferred_element_type=jnp.float32).astype(jnp.bfloat16)
    gate_other = swap_cores(gate_part)
    up_part = jnp.dot(inputs, up_w, preferred_element_type=jnp.float32).astype(jnp.bfloat16)
    up_other = swap_cores(up_part)
    down_w = densify(down_panel[0, 0], down_table)

    own_hidden = activation(whole(gate_part[:own], gate_other[:own]), whole(up_part[:own], up_other[:own]))
    out_part = jnp.dot(own_hidden, down_w, preferred_element_type=jnp.float32).astype(jnp.bfloat16)
    output = f32(out_part[:rows])
    for k in range(1, n_hid):
        output = output + f32(shift(out_part[k * rows : (k + 1) * rows], "hid", k))
    own_slope = ((output - f32(target)) * SLOPE_SCALE).astype(jnp.bfloat16)
    slope = jnp.concatenate(gather_far(gather_near(own_slope)))

    gate_part, gate_other, up_part, up_other, out_part = lax.optimization_barrier(
        (gate_part, gate_other, up_part, up_other, out_part)
    )
    gate = whole(gate_part, gate_other)
    up = whole(up_part, up_other)
    sigmoid_gate = jax.nn.sigmoid(gate)
    silu_gate = gate * sigmoid_gate
    hidden = jnp.concatenate([own_hidden, activation(gate[own:], up[own:])])
    gate_factor = up * sigmoid_gate * (1.0 + gate * (1.0 - sigmoid_gate))
    gate_codes = pick_codes(mine(gate_list), row_blocks, slab_blocks, False)
    up_codes = pick_codes(mine(up_list), row_blocks, slab_blocks, False)
    down_codes = pick_codes(mine(down_list), row_blocks, slab_blocks, True)

    back_part = lax.dot_general(
        slope, down_w, (((1,), (1,)), ((), ())), preferred_element_type=jnp.float32
    ).astype(jnp.bfloat16)
    back_other = swap_cores(back_part)
    down_grad = gradient(hidden, (slope,), down_codes)
    gate_grad = gradient(inputs, (back_part, back_other, gate_factor), gate_codes)
    up_grad = gradient(inputs, (back_part, back_other, silu_gate), up_codes)
    return gate_grad[None, None], up_grad[None, None], down_grad[None, None]


def solution(mesh):
    return jax.shard_map(
        local,
        mesh=mesh,
        in_specs=(
            P(("groups", "hid", "dp"), "col"),
            P(("groups", "hid", "dp"), "col"),
            P(("groups", "hid"), "col", None, None),
            P(("groups", "hid"), "col", None, None),
            P(("groups", "hid"), "col", None, None),
            P(("groups", "hid"), "col", None),
            P(("groups", "hid"), "col", None),
            P(("groups", "hid"), "col", None),
        ),
        out_specs=(
            P(("groups", "hid"), "col", None, "dp"),
            P(("groups", "hid"), "col", None, "dp"),
            P(("groups", "hid"), "col", None, "dp"),
        ),
        check_vma=False,
    )
```

```python
import functools

import jax
import jax.numpy as jnp
from jax import lax
from jax.experimental import pallas as pl
from jax.experimental.pallas import tpu as pltpu
from jax.sharding import PartitionSpec as P

D = 4096
FF = 16384
BLK = 64
PAIR = 2 * BLK
SLOPE_SCALE = 0.0625
DENSIFY_VMEM = 14 * 2**20
PRODUCT_VMEM = 14 * 2**20
GRADIENT_VMEM = 44 * 2**20


def swap_halves(tile):
    return jnp.concatenate([tile[:, BLK:], tile[:, :BLK]], axis=1)


def join(left, right):
    return jnp.concatenate([left[:, :BLK], right[:, BLK:]], axis=1)


def lanes(t):
    return pl.ds(pl.multiple_of(t * PAIR, PAIR), PAIR)


def largest(options, total):
    return max(n for n in options if total % n == 0)


def densify_kernel(half_cap, rows_per_step, n_cols, chunks, table, panel, out, tiles, sems):
    step = pl.program_id(0)
    share = half_cap // chunks

    @pl.when(step == 0)
    def _():
        copies = []
        for c in range(chunks):
            span = pl.ds(c * share * PAIR, share * PAIR)
            copies.append(pltpu.make_async_copy(panel.at[:, span], tiles.at[:, span], sems.at[c]))
            copies[c].start()
        tiles[:, 2 * half_cap * PAIR :] = jnp.zeros((BLK, PAIR), tiles.dtype)
        batch = largest((1, 2, 4, 5, 8), share)
        for c in range(chunks):
            copies[c].wait()

            def stage(b, carry):
                t = c * share + b * batch
                swapped = [swap_halves(tiles[:, lanes(t + u)]) for u in range(batch)]
                for u in range(batch):
                    tiles[:, lanes(half_cap + t + u)] = swapped[u]
                return carry

            lax.fori_loop(0, share // batch, stage, 0)

    def row(i, carry):
        base = (step * rows_per_step + i) * n_cols
        for p in range(n_cols // 2):
            out[pl.ds(pl.multiple_of(i * BLK, BLK), BLK), p * PAIR : (p + 1) * PAIR] = join(
                tiles[:, lanes(table[base + 2 * p])], tiles[:, lanes(table[base + 2 * p + 1])]
            )
        return carry

    lax.fori_loop(0, rows_per_step, row, 0)


def densify(panel, table, n_rows, n_cols):
    half_cap = panel.shape[1] // PAIR
    rows_per_step = max(1, 128 // n_cols)
    chunks = largest((1, 2, 4), half_cap)
    return pl.pallas_call(
        functools.partial(densify_kernel, half_cap, rows_per_step, n_cols, chunks),
        grid_spec=pltpu.PrefetchScalarGridSpec(
            num_scalar_prefetch=1,
            grid=(n_rows // rows_per_step,),
            in_specs=[pl.BlockSpec(memory_space=pltpu.HBM)],
            out_specs=pl.BlockSpec((rows_per_step * BLK, n_cols * BLK), lambda s, *_: (s, 0)),
            scratch_shapes=[
                pltpu.VMEM((BLK, (2 * half_cap + 1) * PAIR), panel.dtype),
                pltpu.SemaphoreType.DMA((chunks,)),
            ],
        ),
        out_shape=jax.ShapeDtypeStruct((n_rows * BLK, n_cols * BLK), panel.dtype),
        compiler_params=pltpu.CompilerParams(vmem_limit_bytes=DENSIFY_VMEM),
        cost_estimate=pl.CostEstimate(
            flops=0, bytes_accessed=4 * panel.size + 4 * n_rows * n_cols * BLK * BLK, transcendentals=0
        ),
        name="densify",
    )(table, panel)


def gradient_kernel(n_steps, rows_per_step, n_cols, n_rhs, picks, lhs, *refs):
    terms, (out, tiles, rows) = refs[:n_rhs], refs[n_rhs : n_rhs + 3]
    step = pl.program_id(0)
    col_pairs = n_cols // 2
    width = 2
    rhs = terms[0]
    if n_rhs == 3:
        rhs = refs[n_rhs + 3]

        @pl.when(step == 0)
        def _():
            mine, theirs, factor = terms

            def scale(j, carry):
                span = pl.ds(pl.multiple_of(j * 2 * PAIR, 2 * PAIR), 2 * PAIR)
                rhs[:, span] = ((f32(mine[:, span]) + f32(theirs[:, span])) * factor[:, span]).astype(rhs.dtype)
                return carry

            lax.fori_loop(0, col_pairs // 2, scale, 0)

    rows[...] = lhs[...].T
    for c in range(0, col_pairs, width):
        part = jnp.dot(
            rows[...], rhs[:, c * PAIR : (c + width) * PAIR], preferred_element_type=jnp.float32
        ).astype(tiles.dtype)
        for i in range(rows_per_step):
            for p in range(width):
                tiles[(step * rows_per_step + i) * col_pairs + c + p] = part[
                    i * BLK : (i + 1) * BLK, p * PAIR : (p + 1) * PAIR
                ]

    @pl.when(step == n_steps - 1)
    def _():
        tiles[n_steps * rows_per_step * col_pairs] = jnp.zeros((BLK, PAIR), tiles.dtype)

        def fetch(code):
            tile = tiles[code // 2]
            return jnp.where(code % 2 == 1, swap_halves(tile), tile)

        def pick(k, carry):
            out[:, lanes(k)] = join(fetch(picks[2 * k]), fetch(picks[2 * k + 1]))
            return carry

        pairs = out.shape[1] // PAIR
        lax.fori_loop(0, pairs, pick, 0, unroll=largest((1, 2, 5, 8), pairs))


def gradient(lhs, terms, picks):
    n_rows, n_cols = lhs.shape[1] // BLK, terms[0].shape[1] // BLK
    rows_per_step = min(16, n_rows)
    n_steps = n_rows // rows_per_step
    scratch = [
        pltpu.VMEM((n_rows * n_cols // 2 + 1, BLK, PAIR), jnp.bfloat16),
        pltpu.VMEM((rows_per_step * BLK, lhs.shape[0]), jnp.bfloat16),
    ]
    if len(terms) == 3:
        scratch.append(pltpu.VMEM(terms[0].shape, jnp.bfloat16))
    return pl.pallas_call(
        functools.partial(gradient_kernel, n_steps, rows_per_step, n_cols, len(terms)),
        grid_spec=pltpu.PrefetchScalarGridSpec(
            num_scalar_prefetch=1,
            grid=(n_steps,),
            in_specs=[pl.BlockSpec((lhs.shape[0], rows_per_step * BLK), lambda s, *_: (0, s))]
            + [pl.BlockSpec(t.shape, lambda s, *_: (0, 0)) for t in terms],
            out_specs=pl.BlockSpec((BLK, picks.shape[0] * BLK), lambda s, *_: (0, 0)),
            scratch_shapes=scratch,
        ),
        out_shape=jax.ShapeDtypeStruct((BLK, picks.shape[0] * BLK), jnp.bfloat16),
        compiler_params=pltpu.CompilerParams(vmem_limit_bytes=GRADIENT_VMEM),
        cost_estimate=pl.CostEstimate(
            flops=2 * lhs.size * terms[0].shape[1],
            bytes_accessed=2 * lhs.size + 4 * len(terms) * terms[0].size + 2 * picks.shape[0] * BLK * BLK,
            transcendentals=0,
        ),
        name="gradient",
    )(picks, lhs, *terms)


def output_kernel(gate_mine, gate_theirs, up_mine, up_theirs, weights, hidden, out):
    @pl.when(pl.program_id(0) == 0)
    def _():
        def act(j, carry):
            span = pl.ds(pl.multiple_of(j * PAIR, PAIR), PAIR)
            hidden[:, span] = activation(
                whole(gate_mine[:, span], gate_theirs[:, span]), whole(up_mine[:, span], up_theirs[:, span])
            )
            return carry

        lax.fori_loop(0, hidden.shape[1] // PAIR, act, 0)

    out[...] = jnp.dot(hidden[...], weights[...], preferred_element_type=jnp.float32).astype(out.dtype)


def hidden_and_output(own, partials, weights):
    depth, width = weights.shape
    part = min(256, width)
    return pl.pallas_call(
        output_kernel,
        grid=(width // part,),
        in_specs=[pl.BlockSpec((own, depth), lambda s: (0, 0), pipeline_mode=pl.Buffered(1))] * 4
        + [pl.BlockSpec((depth, part), lambda s: (0, s))],
        out_specs=[
            pl.BlockSpec((own, depth), lambda s: (0, 0)),
            pl.BlockSpec((own, part), lambda s: (0, s)),
        ],
        out_shape=[
            jax.ShapeDtypeStruct((own, depth), jnp.bfloat16),
            jax.ShapeDtypeStruct((own, width), jnp.bfloat16),
        ],
        compiler_params=pltpu.CompilerParams(vmem_limit_bytes=PRODUCT_VMEM),
        cost_estimate=pl.CostEstimate(
            flops=2 * own * depth * width,
            bytes_accessed=2 * (5 * own * depth + depth * width + own * width),
            transcendentals=own * depth,
        ),
        name="output",
    )(*partials, weights)


def back_kernel(slope, weights, out):
    out[...] = lax.dot_general(
        slope[...], weights[...], (((1,), (1,)), ((), ())), preferred_element_type=jnp.float32
    ).astype(out.dtype)


def back_product(slope, weights):
    width, depth = weights.shape
    rows = slope.shape[0]
    part = min(512, width)
    return pl.pallas_call(
        back_kernel,
        grid=(width // part,),
        in_specs=[
            pl.BlockSpec((rows, depth), lambda s: (0, 0)),
            pl.BlockSpec((part, depth), lambda s: (s, 0)),
        ],
        out_specs=pl.BlockSpec((rows, part), lambda s: (0, s)),
        out_shape=jax.ShapeDtypeStruct((rows, width), jnp.bfloat16),
        compiler_params=pltpu.CompilerParams(vmem_limit_bytes=PRODUCT_VMEM),
        cost_estimate=pl.CostEstimate(
            flops=2 * rows * depth * width,
            bytes_accessed=2 * (rows * depth + depth * width + rows * width),
            transcendentals=0,
        ),
        name="back",
    )(slope, weights)


def tile_table(block_ids, row_blocks, slab_blocks, rows_are_hidden):
    cap = block_ids.shape[0]
    grid = row_blocks * slab_blocks
    slot = jnp.arange(1, cap + 1, dtype=jnp.int32)
    held = jnp.sum(
        jnp.where(block_ids[None, :] == jnp.arange(grid, dtype=jnp.int32)[:, None], slot[None, :], 0), axis=1
    )
    held = held.reshape(row_blocks, slab_blocks)
    if rows_are_hidden:
        held = held.T
    half = jnp.arange(held.shape[1], dtype=jnp.int32)[None, :] % 2
    index = held - 1
    tile = index // 2 + jnp.where(index % 2 != half, cap // 2, 0)
    return jnp.where(held > 0, tile, cap).reshape(-1)


def pick_codes(block_ids, row_blocks, slab_blocks, rows_are_hidden):
    grid = row_blocks * slab_blocks
    row, col = block_ids // slab_blocks, block_ids % slab_blocks
    cols = slab_blocks
    if rows_are_hidden:
        row, col, cols = col, row, row_blocks
    half = jnp.arange(block_ids.shape[0], dtype=jnp.int32) % 2
    code = 2 * (row * (cols // 2) + col // 2) + jnp.where(col % 2 != half, 1, 0)
    return jnp.where(block_ids < grid, code, grid)


def shift(values, axis, k):
    n = lax.axis_size(axis)
    return values if k == 0 else lax.ppermute(values, axis, [(i, i ^ k) for i in range(n)])


def gather_near(values):
    return [shift(values, "hid", k) for k in range(lax.axis_size("hid"))]


def gather_far(near):
    far = [shift(v, "dp", j) for j in range(1, lax.axis_size("dp")) for v in near]
    return near + far


def swap_cores(values):
    return lax.ppermute(values, "col", [(0, 1), (1, 0)])


def f32(values):
    return values.astype(jnp.float32)


def whole(mine, theirs):
    return f32(mine) + f32(theirs)


def activation(gate, up):
    return (gate * jax.nn.sigmoid(gate) * up).astype(jnp.bfloat16)


def local(tokens, target, gate_panel, up_panel, down_panel, gate_list, up_list, down_list):
    n_hid, n_dp = lax.axis_size("hid"), lax.axis_size("dp")
    slab_blocks = FF // BLK // n_hid
    row_blocks = D // BLK // lax.axis_size("col")
    rows = tokens.shape[0]
    own = rows * n_hid

    def mine(block_list):
        share = block_list.shape[-1] // n_dp
        return lax.dynamic_slice_in_dim(block_list[0, 0], lax.axis_index("dp") * share, share)

    tables = (
        tile_table(gate_list[0, 0], row_blocks, slab_blocks, False),
        tile_table(up_list[0, 0], row_blocks, slab_blocks, False),
        tile_table(down_list[0, 0], row_blocks, slab_blocks, True),
        pick_codes(mine(gate_list), row_blocks, slab_blocks, False),
        pick_codes(mine(up_list), row_blocks, slab_blocks, False),
        pick_codes(mine(down_list), row_blocks, slab_blocks, True),
    )
    tables, gate_panel = lax.optimization_barrier((tables, gate_panel))
    gate_table, up_table, down_table, gate_codes, up_codes, down_codes = tables

    near = gather_near(tokens)
    gate_w = densify(gate_panel[0, 0], gate_table, row_blocks, slab_blocks)
    near, gate_w = lax.optimization_barrier((near, gate_w))
    inputs = jnp.concatenate(gather_far(near))

    gate_part = jnp.dot(inputs, gate_w, preferred_element_type=jnp.float32).astype(jnp.bfloat16)
    gate_other = swap_cores(gate_part)
    up_table, gate_part = lax.optimization_barrier((up_table, gate_part))
    up_w = densify(up_panel[0, 0], up_table, row_blocks, slab_blocks)
    up_part = jnp.dot(inputs, up_w, preferred_element_type=jnp.float32).astype(jnp.bfloat16)
    up_other = swap_cores(up_part)
    down_w = densify(down_panel[0, 0], down_table, slab_blocks, row_blocks)

    partials = (gate_part, gate_other, up_part, up_other)
    own_hidden, out_part = hidden_and_output(own, partials, down_w)
    sent = [out_part[k * rows : (k + 1) * rows] for k in range(n_hid)]
    moved = [shift(sent[k], "hid", k) for k in range(n_hid)]

    partials, own_hidden, out_part, down_table = lax.optimization_barrier(
        (partials, own_hidden, out_part, down_table)
    )
    down_w = densify(down_panel[0, 0], down_table, slab_blocks, row_blocks)
    gate = whole(*partials[:2])
    up = whole(*partials[2:])
    sigmoid_gate = jax.nn.sigmoid(gate)
    silu_gate = gate * sigmoid_gate
    hidden = jnp.concatenate([own_hidden, activation(gate[own:], up[own:])])
    gate_factor = up * sigmoid_gate * (1.0 + gate * (1.0 - sigmoid_gate))
    moved, down_w, silu_gate, hidden, gate_factor = lax.optimization_barrier(
        (moved, down_w, silu_gate, hidden, gate_factor)
    )

    output = f32(moved[0])
    for k in range(1, n_hid):
        output = output + f32(moved[k])
    own_slope = ((output - f32(target)) * SLOPE_SCALE).astype(jnp.bfloat16)
    slope = jnp.concatenate(gather_far(gather_near(own_slope)))
    back_part = back_product(slope, down_w)
    back_other = swap_cores(back_part)
    down_grad = gradient(hidden, (slope,), down_codes)
    gate_grad = gradient(inputs, (back_part, back_other, gate_factor), gate_codes)
    up_grad = gradient(inputs, (back_part, back_other, silu_gate), up_codes)
    return gate_grad[None, None], up_grad[None, None], down_grad[None, None]


def solution(mesh):
    return jax.shard_map(
        local,
        mesh=mesh,
        in_specs=(
            P(("groups", "hid", "dp"), "col"),
            P(("groups", "hid", "dp"), "col"),
            P(("groups", "hid"), "col", None, None),
            P(("groups", "hid"), "col", None, None),
            P(("groups", "hid"), "col", None, None),
            P(("groups", "hid"), "col", None),
            P(("groups", "hid"), "col", None),
            P(("groups", "hid"), "col", None),
        ),
        out_specs=(
            P(("groups", "hid"), "col", None, "dp"),
            P(("groups", "hid"), "col", None, "dp"),
            P(("groups", "hid"), "col", None, "dp"),
        ),
        check_vma=False,
    )
```

```python
import functools

import jax
import jax.numpy as jnp
from jax import lax
from jax.experimental import pallas as pl
from jax.experimental.pallas import tpu as pltpu
from jax.sharding import PartitionSpec as P

D = 4096
FF = 16384
BLK = 64
PAIR = 2 * BLK
SLOPE_SCALE = 0.0625
DENSIFY_VMEM = 14 * 2**20
PRODUCT_VMEM = 14 * 2**20
GRADIENT_VMEM = 44 * 2**20


def swap_halves(tile):
    return jnp.concatenate([tile[:, BLK:], tile[:, :BLK]], axis=1)


def join(left, right):
    return jnp.concatenate([left[:, :BLK], right[:, BLK:]], axis=1)


def lanes(t):
    return pl.ds(pl.multiple_of(t * PAIR, PAIR), PAIR)


def largest(options, total):
    return max(n for n in options if total % n == 0)


def densify_kernel(half_cap, rows_per_step, n_cols, chunks, table, panel, out, tiles, sems):
    step = pl.program_id(0)
    share = half_cap // chunks

    @pl.when(step == 0)
    def _():
        copies = []
        for c in range(chunks):
            span = pl.ds(c * share * PAIR, share * PAIR)
            copies.append(pltpu.make_async_copy(panel.at[:, span], tiles.at[:, span], sems.at[c]))
            copies[c].start()
        tiles[:, 2 * half_cap * PAIR :] = jnp.zeros((BLK, PAIR), tiles.dtype)
        batch = largest((1, 2, 4, 5, 8, 10, 16, 20, 40), share)
        for c in range(chunks):
            copies[c].wait()

            def stage(b, carry):
                t = c * share + b * batch
                swapped = [swap_halves(tiles[:, lanes(t + u)]) for u in range(batch)]
                for u in range(batch):
                    tiles[:, lanes(half_cap + t + u)] = swapped[u]
                return carry

            lax.fori_loop(0, share // batch, stage, 0)

    def row(i, carry):
        base = (step * rows_per_step + i) * n_cols
        for p in range(n_cols // 2):
            out[pl.ds(pl.multiple_of(i * BLK, BLK), BLK), p * PAIR : (p + 1) * PAIR] = join(
                tiles[:, lanes(table[base + 2 * p])], tiles[:, lanes(table[base + 2 * p + 1])]
            )
        return carry

    lax.fori_loop(0, rows_per_step, row, 0)


def densify(panel, table, n_rows, n_cols):
    half_cap = panel.shape[1] // PAIR
    rows_per_step = max(1, 128 // n_cols)
    chunks = largest((1, 2, 4), half_cap)
    return pl.pallas_call(
        functools.partial(densify_kernel, half_cap, rows_per_step, n_cols, chunks),
        grid_spec=pltpu.PrefetchScalarGridSpec(
            num_scalar_prefetch=1,
            grid=(n_rows // rows_per_step,),
            in_specs=[pl.BlockSpec(memory_space=pltpu.HBM)],
            out_specs=pl.BlockSpec((rows_per_step * BLK, n_cols * BLK), lambda s, *_: (s, 0)),
            scratch_shapes=[
                pltpu.VMEM((BLK, (2 * half_cap + 1) * PAIR), panel.dtype),
                pltpu.SemaphoreType.DMA((chunks,)),
            ],
        ),
        out_shape=jax.ShapeDtypeStruct((n_rows * BLK, n_cols * BLK), panel.dtype),
        compiler_params=pltpu.CompilerParams(vmem_limit_bytes=DENSIFY_VMEM),
        cost_estimate=pl.CostEstimate(
            flops=0, bytes_accessed=4 * panel.size + 4 * n_rows * n_cols * BLK * BLK, transcendentals=0
        ),
        name="densify",
    )(table, pltpu.with_memory_space_constraint(panel, pltpu.HBM))


def gradient_kernel(n_steps, rows_per_step, n_cols, n_rhs, picks, lhs, *refs):
    terms, (out, tiles, rows) = refs[:n_rhs], refs[n_rhs : n_rhs + 3]
    step = pl.program_id(0)
    col_pairs = n_cols // 2
    width = 2
    rhs = terms[0]
    if n_rhs == 3:
        rhs = refs[n_rhs + 3]

        @pl.when(step == 0)
        def _():
            mine, theirs, factor = terms

            def scale(j, carry):
                span = pl.ds(pl.multiple_of(j * 2 * PAIR, 2 * PAIR), 2 * PAIR)
                rhs[:, span] = ((f32(mine[:, span]) + f32(theirs[:, span])) * factor[:, span]).astype(rhs.dtype)
                return carry

            lax.fori_loop(0, col_pairs // 2, scale, 0)

    rows[...] = lhs[...].T
    for c in range(0, col_pairs, width):
        part = jnp.dot(
            rows[...], rhs[:, c * PAIR : (c + width) * PAIR], preferred_element_type=jnp.float32
        ).astype(tiles.dtype)
        for i in range(rows_per_step):
            for p in range(width):
                tiles[(step * rows_per_step + i) * col_pairs + c + p] = part[
                    i * BLK : (i + 1) * BLK, p * PAIR : (p + 1) * PAIR
                ]

    @pl.when(step == n_steps - 1)
    def _():
        tiles[n_steps * rows_per_step * col_pairs] = jnp.zeros((BLK, PAIR), tiles.dtype)

        def pair(first, second):
            left, right = tiles[first >> 1], tiles[second >> 1]
            turn_left, turn_right = (first & 1) == 1, (second & 1) == 1
            turned = swap_halves(jnp.where(turn_left, jnp.where(turn_right, join(right, left), left), right))
            return join(jnp.where(turn_left, turned, left), jnp.where(turn_right, turned, right))

        pairs = out.shape[1] // PAIR
        batch = largest((1, 2, 5, 8, 10, 16), pairs)

        def pick(b, carry):
            k = b * batch
            kept = [pair(picks[2 * (k + u)], picks[2 * (k + u) + 1]) for u in range(batch)]
            for u in range(batch):
                out[:, lanes(k + u)] = kept[u]
            return carry

        lax.fori_loop(0, pairs // batch, pick, 0)


def gradient(lhs, terms, picks):
    n_rows, n_cols = lhs.shape[1] // BLK, terms[0].shape[1] // BLK
    rows_per_step = min(16, n_rows)
    n_steps = n_rows // rows_per_step
    scratch = [
        pltpu.VMEM((n_rows * n_cols // 2 + 1, BLK, PAIR), jnp.bfloat16),
        pltpu.VMEM((rows_per_step * BLK, lhs.shape[0]), jnp.bfloat16),
    ]
    if len(terms) == 3:
        scratch.append(pltpu.VMEM(terms[0].shape, jnp.bfloat16))
    return pl.pallas_call(
        functools.partial(gradient_kernel, n_steps, rows_per_step, n_cols, len(terms)),
        grid_spec=pltpu.PrefetchScalarGridSpec(
            num_scalar_prefetch=1,
            grid=(n_steps,),
            in_specs=[pl.BlockSpec((lhs.shape[0], rows_per_step * BLK), lambda s, *_: (0, s))]
            + [pl.BlockSpec(t.shape, lambda s, *_: (0, 0)) for t in terms],
            out_specs=pl.BlockSpec((BLK, picks.shape[0] * BLK), lambda s, *_: (0, 0)),
            scratch_shapes=scratch,
        ),
        out_shape=jax.ShapeDtypeStruct((BLK, picks.shape[0] * BLK), jnp.bfloat16),
        compiler_params=pltpu.CompilerParams(vmem_limit_bytes=GRADIENT_VMEM),
        cost_estimate=pl.CostEstimate(
            flops=2 * lhs.size * terms[0].shape[1],
            bytes_accessed=2 * lhs.size + 4 * len(terms) * terms[0].size + 2 * picks.shape[0] * BLK * BLK,
            transcendentals=0,
        ),
        name="gradient",
    )(picks, lhs, *terms)


def output_kernel(gate_mine, gate_theirs, up_mine, up_theirs, weights, hidden, out):
    @pl.when(pl.program_id(0) == 0)
    def _():
        def act(j, carry):
            span = pl.ds(pl.multiple_of(j * 2 * PAIR, 2 * PAIR), 2 * PAIR)
            hidden[:, span] = activation(
                whole(gate_mine[:, span], gate_theirs[:, span]), whole(up_mine[:, span], up_theirs[:, span])
            )
            return carry

        lax.fori_loop(0, hidden.shape[1] // (2 * PAIR), act, 0)

    out[...] = jnp.dot(hidden[...], weights[...], preferred_element_type=jnp.float32).astype(out.dtype)


def hidden_and_output(own, partials, weights):
    depth, width = weights.shape
    part = min(256, width)
    return pl.pallas_call(
        output_kernel,
        grid=(width // part,),
        in_specs=[pl.BlockSpec((own, depth), lambda s: (0, 0), pipeline_mode=pl.Buffered(1))] * 4
        + [pl.BlockSpec((depth, part), lambda s: (0, s))],
        out_specs=[
            pl.BlockSpec((own, depth), lambda s: (0, 0)),
            pl.BlockSpec((own, part), lambda s: (0, s)),
        ],
        out_shape=[
            jax.ShapeDtypeStruct((own, depth), jnp.bfloat16),
            jax.ShapeDtypeStruct((own, width), jnp.bfloat16),
        ],
        compiler_params=pltpu.CompilerParams(vmem_limit_bytes=PRODUCT_VMEM),
        cost_estimate=pl.CostEstimate(
            flops=2 * own * depth * width,
            bytes_accessed=2 * (5 * own * depth + depth * width + own * width),
            transcendentals=own * depth,
        ),
        name="output",
    )(*partials, weights)


def back_kernel(slope, weights, out):
    out[...] = lax.dot_general(
        slope[...], weights[...], (((1,), (1,)), ((), ())), preferred_element_type=jnp.float32
    ).astype(out.dtype)


def back_product(slope, weights):
    width, depth = weights.shape
    rows = slope.shape[0]
    part = min(512, width)
    return pl.pallas_call(
        back_kernel,
        grid=(width // part,),
        in_specs=[
            pl.BlockSpec((rows, depth), lambda s: (0, 0)),
            pl.BlockSpec((part, depth), lambda s: (s, 0)),
        ],
        out_specs=pl.BlockSpec((rows, part), lambda s: (0, s)),
        out_shape=jax.ShapeDtypeStruct((rows, width), jnp.bfloat16),
        compiler_params=pltpu.CompilerParams(vmem_limit_bytes=PRODUCT_VMEM),
        cost_estimate=pl.CostEstimate(
            flops=2 * rows * depth * width,
            bytes_accessed=2 * (rows * depth + depth * width + rows * width),
            transcendentals=0,
        ),
        name="back",
    )(slope, weights)


def tile_table(block_ids, row_blocks, slab_blocks, rows_are_hidden):
    cap = block_ids.shape[0]
    grid = row_blocks * slab_blocks
    slot = jnp.arange(1, cap + 1, dtype=jnp.int32)
    held = jnp.sum(
        jnp.where(block_ids[None, :] == jnp.arange(grid, dtype=jnp.int32)[:, None], slot[None, :], 0), axis=1
    )
    held = held.reshape(row_blocks, slab_blocks)
    if rows_are_hidden:
        held = held.T
    half = jnp.arange(held.shape[1], dtype=jnp.int32)[None, :] % 2
    index = held - 1
    tile = index // 2 + jnp.where(index % 2 != half, cap // 2, 0)
    return jnp.where(held > 0, tile, cap).reshape(-1)


def pick_codes(block_ids, row_blocks, slab_blocks, rows_are_hidden):
    grid = row_blocks * slab_blocks
    row, col = block_ids // slab_blocks, block_ids % slab_blocks
    cols = slab_blocks
    if rows_are_hidden:
        row, col, cols = col, row, row_blocks
    half = jnp.arange(block_ids.shape[0], dtype=jnp.int32) % 2
    code = 2 * (row * (cols // 2) + col // 2) + jnp.where(col % 2 != half, 1, 0)
    return jnp.where(block_ids < grid, code, grid)


def shift(values, axis, k):
    n = lax.axis_size(axis)
    return values if k == 0 else lax.ppermute(values, axis, [(i, i ^ k) for i in range(n)])


def gather_near(values):
    return [shift(values, "hid", k) for k in range(lax.axis_size("hid"))]


def gather_far(near):
    far = [shift(v, "dp", j) for j in range(1, lax.axis_size("dp")) for v in near]
    return near + far


def swap_cores(values):
    return lax.ppermute(values, "col", [(0, 1), (1, 0)])


def f32(values):
    return values.astype(jnp.float32)


def whole(mine, theirs):
    return f32(mine) + f32(theirs)


def activation(gate, up):
    return (gate * jax.nn.sigmoid(gate) * up).astype(jnp.bfloat16)


def local(tokens, target, gate_panel, up_panel, down_panel, gate_list, up_list, down_list):
    n_hid, n_dp = lax.axis_size("hid"), lax.axis_size("dp")
    slab_blocks = FF // BLK // n_hid
    row_blocks = D // BLK // lax.axis_size("col")
    rows = tokens.shape[0]
    own = rows * n_hid

    def mine(block_list):
        share = block_list.shape[-1] // n_dp
        return lax.dynamic_slice_in_dim(block_list[0, 0], lax.axis_index("dp") * share, share)

    tables = (
        tile_table(gate_list[0, 0], row_blocks, slab_blocks, False),
        tile_table(up_list[0, 0], row_blocks, slab_blocks, False),
        tile_table(down_list[0, 0], row_blocks, slab_blocks, True),
        pick_codes(mine(gate_list), row_blocks, slab_blocks, False),
        pick_codes(mine(up_list), row_blocks, slab_blocks, False),
        pick_codes(mine(down_list), row_blocks, slab_blocks, True),
    )
    tables, gate_panel = lax.optimization_barrier((tables, gate_panel))
    gate_table, up_table, down_table, gate_codes, up_codes, down_codes = tables

    near, gate_table = lax.optimization_barrier((gather_near(tokens), gate_table))
    gate_w = densify(gate_panel[0, 0], gate_table, row_blocks, slab_blocks)
    inputs = jnp.concatenate(gather_far(near))

    gate_part = jnp.dot(inputs, gate_w, preferred_element_type=jnp.float32).astype(jnp.bfloat16)
    gate_other = swap_cores(gate_part)
    up_table, gate_part = lax.optimization_barrier((up_table, gate_part))
    up_w = densify(up_panel[0, 0], up_table, row_blocks, slab_blocks)
    up_part = jnp.dot(inputs, up_w, preferred_element_type=jnp.float32).astype(jnp.bfloat16)
    up_other = swap_cores(up_part)
    down_w = densify(down_panel[0, 0], down_table, slab_blocks, row_blocks)

    partials = (gate_part, gate_other, up_part, up_other)
    own_hidden, out_part = hidden_and_output(own, partials, down_w)
    sent = [out_part[k * rows : (k + 1) * rows] for k in range(n_hid)]
    moved = [shift(sent[k], "hid", k) for k in range(n_hid)]

    partials, own_hidden, out_part = lax.optimization_barrier((partials, own_hidden, out_part))
    gate = whole(*partials[:2])
    up = whole(*partials[2:])
    sigmoid_gate = jax.nn.sigmoid(gate)
    silu_gate = gate * sigmoid_gate
    hidden = jnp.concatenate([own_hidden, activation(gate[own:], up[own:])])
    gate_factor = up * sigmoid_gate * (1.0 + gate * (1.0 - sigmoid_gate))
    moved, silu_gate, hidden, gate_factor = lax.optimization_barrier(
        (moved, silu_gate, hidden, gate_factor)
    )

    output = f32(moved[0])
    for k in range(1, n_hid):
        output = output + f32(moved[k])
    own_slope = ((output - f32(target)) * SLOPE_SCALE).astype(jnp.bfloat16)
    slope = jnp.concatenate(gather_far(gather_near(own_slope)))
    back_part = back_product(slope, down_w)
    back_other = swap_cores(back_part)
    down_grad = gradient(hidden, (slope,), down_codes)
    gate_grad = gradient(inputs, (back_part, back_other, gate_factor), gate_codes)
    up_grad = gradient(inputs, (back_part, back_other, silu_gate), up_codes)
    return gate_grad[None, None], up_grad[None, None], down_grad[None, None]


def solution(mesh):
    return jax.shard_map(
        local,
        mesh=mesh,
        in_specs=(
            P(("groups", "hid", "dp"), "col"),
            P(("groups", "hid", "dp"), "col"),
            P(("groups", "hid"), "col", None, None),
            P(("groups", "hid"), "col", None, None),
            P(("groups", "hid"), "col", None, None),
            P(("groups", "hid"), "col", None),
            P(("groups", "hid"), "col", None),
            P(("groups", "hid"), "col", None),
        ),
        out_specs=(
            P(("groups", "hid"), "col", None, "dp"),
            P(("groups", "hid"), "col", None, "dp"),
            P(("groups", "hid"), "col", None, "dp"),
        ),
        check_vma=False,
    )
```

```python
import functools

import jax
import jax.numpy as jnp
from jax import lax
from jax.experimental import pallas as pl
from jax.experimental.pallas import tpu as pltpu
from jax.sharding import PartitionSpec as P

D = 4096
FF = 16384
BLK = 64
PAIR = 2 * BLK
SLOPE_SCALE = 0.0625
DENSIFY_VMEM = 14 * 2**20
PRODUCT_VMEM = 14 * 2**20
DEPTH_PART = 512
GRADIENT_VMEM = 44 * 2**20


def swap_halves(tile):
    return jnp.concatenate([tile[:, BLK:], tile[:, :BLK]], axis=1)


def join(left, right):
    return jnp.concatenate([left[:, :BLK], right[:, BLK:]], axis=1)


def lanes(t):
    return pl.ds(pl.multiple_of(t * PAIR, PAIR), PAIR)


def largest(options, total):
    return max(n for n in options if total % n == 0)


def densify_kernel(half_cap, rows_per_step, n_cols, chunks, table, panel, out, tiles, sems):
    step = pl.program_id(0)
    share = half_cap // chunks

    @pl.when(step == 0)
    def _():
        copies = []
        for c in range(chunks):
            span = pl.ds(c * share * PAIR, share * PAIR)
            copies.append(pltpu.make_async_copy(panel.at[:, span], tiles.at[:, span], sems.at[c]))
            copies[c].start()
        tiles[:, 2 * half_cap * PAIR :] = jnp.zeros((BLK, PAIR), tiles.dtype)
        batch = largest((1, 2, 4, 5, 8, 10, 16, 20, 40), share)
        for c in range(chunks):
            copies[c].wait()

            def stage(b, carry):
                t = c * share + b * batch
                swapped = [swap_halves(tiles[:, lanes(t + u)]) for u in range(batch)]
                for u in range(batch):
                    tiles[:, lanes(half_cap + t + u)] = swapped[u]
                return carry

            lax.fori_loop(0, share // batch, stage, 0)

    def row(i, carry):
        base = (step * rows_per_step + i) * n_cols
        for p in range(n_cols // 2):
            out[pl.ds(pl.multiple_of(i * BLK, BLK), BLK), p * PAIR : (p + 1) * PAIR] = join(
                tiles[:, lanes(table[base + 2 * p])], tiles[:, lanes(table[base + 2 * p + 1])]
            )
        return carry

    lax.fori_loop(0, rows_per_step, row, 0)


def densify(panel, table, n_rows, n_cols):
    half_cap = panel.shape[1] // PAIR
    rows_per_step = max(1, 128 // n_cols)
    chunks = largest((1, 2, 4), half_cap)
    return pl.pallas_call(
        functools.partial(densify_kernel, half_cap, rows_per_step, n_cols, chunks),
        grid_spec=pltpu.PrefetchScalarGridSpec(
            num_scalar_prefetch=1,
            grid=(n_rows // rows_per_step,),
            in_specs=[pl.BlockSpec(memory_space=pltpu.HBM)],
            out_specs=pl.BlockSpec((rows_per_step * BLK, n_cols * BLK), lambda s, *_: (s, 0)),
            scratch_shapes=[
                pltpu.VMEM((BLK, (2 * half_cap + 1) * PAIR), panel.dtype),
                pltpu.SemaphoreType.DMA((chunks,)),
            ],
        ),
        out_shape=jax.ShapeDtypeStruct((n_rows * BLK, n_cols * BLK), panel.dtype),
        compiler_params=pltpu.CompilerParams(vmem_limit_bytes=DENSIFY_VMEM),
        cost_estimate=pl.CostEstimate(
            flops=0, bytes_accessed=4 * panel.size + 4 * n_rows * n_cols * BLK * BLK, transcendentals=0
        ),
        name="densify",
    )(table, pltpu.with_memory_space_constraint(panel, pltpu.HBM))


def gradient_kernel(n_steps, rows_per_step, n_cols, n_rhs, picks, lhs, *refs):
    terms, (out, tiles, rows) = refs[:n_rhs], refs[n_rhs : n_rhs + 3]
    step = pl.program_id(0)
    col_pairs = n_cols // 2
    width = 2
    rhs = terms[0]
    if n_rhs == 3:
        rhs = refs[n_rhs + 3]

        @pl.when(step == 0)
        def _():
            mine, theirs, factor = terms

            def scale(j, carry):
                span = pl.ds(pl.multiple_of(j * 2 * PAIR, 2 * PAIR), 2 * PAIR)
                rhs[:, span] = ((f32(mine[:, span]) + f32(theirs[:, span])) * factor[:, span]).astype(rhs.dtype)
                return carry

            lax.fori_loop(0, col_pairs // 2, scale, 0)

    rows[...] = lhs[...].T
    for c in range(0, col_pairs, width):
        part = jnp.dot(
            rows[...], rhs[:, c * PAIR : (c + width) * PAIR], preferred_element_type=jnp.float32
        ).astype(tiles.dtype)
        for i in range(rows_per_step):
            for p in range(width):
                tiles[(step * rows_per_step + i) * col_pairs + c + p] = part[
                    i * BLK : (i + 1) * BLK, p * PAIR : (p + 1) * PAIR
                ]

    @pl.when(step == n_steps - 1)
    def _():
        tiles[n_steps * rows_per_step * col_pairs] = jnp.zeros((BLK, PAIR), tiles.dtype)

        def pair(first, second):
            left, right = tiles[first >> 1], tiles[second >> 1]
            turn_left, turn_right = (first & 1) == 1, (second & 1) == 1
            turned = swap_halves(jnp.where(turn_left, jnp.where(turn_right, join(right, left), left), right))
            return join(jnp.where(turn_left, turned, left), jnp.where(turn_right, turned, right))

        pairs = out.shape[1] // PAIR
        batch = largest((1, 2, 5, 8, 10, 16), pairs)

        def pick(b, carry):
            k = b * batch
            kept = [pair(picks[2 * (k + u)], picks[2 * (k + u) + 1]) for u in range(batch)]
            for u in range(batch):
                out[:, lanes(k + u)] = kept[u]
            return carry

        lax.fori_loop(0, pairs // batch, pick, 0)


def gradient(lhs, terms, picks):
    n_rows, n_cols = lhs.shape[1] // BLK, terms[0].shape[1] // BLK
    rows_per_step = min(16, n_rows)
    n_steps = n_rows // rows_per_step
    scratch = [
        pltpu.VMEM((n_rows * n_cols // 2 + 1, BLK, PAIR), jnp.bfloat16),
        pltpu.VMEM((rows_per_step * BLK, lhs.shape[0]), jnp.bfloat16),
    ]
    if len(terms) == 3:
        scratch.append(pltpu.VMEM(terms[0].shape, jnp.bfloat16))
    return pl.pallas_call(
        functools.partial(gradient_kernel, n_steps, rows_per_step, n_cols, len(terms)),
        grid_spec=pltpu.PrefetchScalarGridSpec(
            num_scalar_prefetch=1,
            grid=(n_steps,),
            in_specs=[pl.BlockSpec((lhs.shape[0], rows_per_step * BLK), lambda s, *_: (0, s))]
            + [pl.BlockSpec(t.shape, lambda s, *_: (0, 0)) for t in terms],
            out_specs=pl.BlockSpec((BLK, picks.shape[0] * BLK), lambda s, *_: (0, 0)),
            scratch_shapes=scratch,
        ),
        out_shape=jax.ShapeDtypeStruct((BLK, picks.shape[0] * BLK), jnp.bfloat16),
        compiler_params=pltpu.CompilerParams(vmem_limit_bytes=GRADIENT_VMEM),
        cost_estimate=pl.CostEstimate(
            flops=2 * lhs.size * terms[0].shape[1],
            bytes_accessed=2 * lhs.size + 4 * len(terms) * terms[0].size + 2 * picks.shape[0] * BLK * BLK,
            transcendentals=0,
        ),
        name="gradient",
    )(picks, lhs, *terms)


def output_kernel(gate_mine, gate_theirs, up_mine, up_theirs, weights, hidden, out, total):
    step = pl.program_id(0)
    hidden[...] = activation(whole(gate_mine[...], gate_theirs[...]), whole(up_mine[...], up_theirs[...]))
    term = jnp.dot(hidden[...], weights[...], preferred_element_type=jnp.float32)

    @pl.when(step == 0)
    def _():
        total[...] = term

    @pl.when(step > 0)
    def _():
        total[...] += term

    @pl.when(step == pl.num_programs(0) - 1)
    def _():
        out[...] = total[...].astype(out.dtype)


def hidden_and_output(own, partials, weights):
    depth, width = weights.shape
    part = min(DEPTH_PART, depth)
    return pl.pallas_call(
        output_kernel,
        grid=(depth // part,),
        in_specs=[pl.BlockSpec((own, part), lambda s: (0, s))] * 4
        + [pl.BlockSpec((part, width), lambda s: (s, 0))],
        out_specs=[
            pl.BlockSpec((own, part), lambda s: (0, s)),
            pl.BlockSpec((own, width), lambda s: (0, 0)),
        ],
        out_shape=[
            jax.ShapeDtypeStruct((own, depth), jnp.bfloat16),
            jax.ShapeDtypeStruct((own, width), jnp.bfloat16),
        ],
        scratch_shapes=[pltpu.VMEM((own, width), jnp.float32)],
        compiler_params=pltpu.CompilerParams(vmem_limit_bytes=PRODUCT_VMEM),
        cost_estimate=pl.CostEstimate(
            flops=2 * own * depth * width,
            bytes_accessed=2 * (5 * own * depth + depth * width + own * width),
            transcendentals=own * depth,
        ),
        name="output",
    )(*partials, weights)


def back_kernel(slope, weights, out):
    out[...] = lax.dot_general(
        slope[...], weights[...], (((1,), (1,)), ((), ())), preferred_element_type=jnp.float32
    ).astype(out.dtype)


def back_product(slope, weights):
    width, depth = weights.shape
    rows = slope.shape[0]
    part = min(512, width)
    return pl.pallas_call(
        back_kernel,
        grid=(width // part,),
        in_specs=[
            pl.BlockSpec((rows, depth), lambda s: (0, 0)),
            pl.BlockSpec((part, depth), lambda s: (s, 0)),
        ],
        out_specs=pl.BlockSpec((rows, part), lambda s: (0, s)),
        out_shape=jax.ShapeDtypeStruct((rows, width), jnp.bfloat16),
        compiler_params=pltpu.CompilerParams(vmem_limit_bytes=PRODUCT_VMEM),
        cost_estimate=pl.CostEstimate(
            flops=2 * rows * depth * width,
            bytes_accessed=2 * (rows * depth + depth * width + rows * width),
            transcendentals=0,
        ),
        name="back",
    )(slope, weights)


def tile_table(block_ids, row_blocks, slab_blocks, rows_are_hidden):
    cap = block_ids.shape[0]
    grid = row_blocks * slab_blocks
    slot = jnp.arange(1, cap + 1, dtype=jnp.int32)
    held = jnp.sum(
        jnp.where(block_ids[None, :] == jnp.arange(grid, dtype=jnp.int32)[:, None], slot[None, :], 0), axis=1
    )
    held = held.reshape(row_blocks, slab_blocks)
    if rows_are_hidden:
        held = held.T
    half = jnp.arange(held.shape[1], dtype=jnp.int32)[None, :] % 2
    index = held - 1
    tile = index // 2 + jnp.where(index % 2 != half, cap // 2, 0)
    return jnp.where(held > 0, tile, cap).reshape(-1)


def pick_codes(block_ids, row_blocks, slab_blocks, rows_are_hidden):
    grid = row_blocks * slab_blocks
    row, col = block_ids // slab_blocks, block_ids % slab_blocks
    cols = slab_blocks
    if rows_are_hidden:
        row, col, cols = col, row, row_blocks
    half = jnp.arange(block_ids.shape[0], dtype=jnp.int32) % 2
    code = 2 * (row * (cols // 2) + col // 2) + jnp.where(col % 2 != half, 1, 0)
    return jnp.where(block_ids < grid, code, grid)


def shift(values, axis, k):
    n = lax.axis_size(axis)
    return values if k == 0 else lax.ppermute(values, axis, [(i, i ^ k) for i in range(n)])


def gather_near(values):
    return [shift(values, "hid", k) for k in range(lax.axis_size("hid"))]


def gather_far(near):
    far = [shift(v, "dp", j) for j in range(1, lax.axis_size("dp")) for v in near]
    return near + far


def swap_cores(values):
    return lax.ppermute(values, "col", [(0, 1), (1, 0)])


def f32(values):
    return values.astype(jnp.float32)


def whole(mine, theirs):
    return f32(mine) + f32(theirs)


def activation(gate, up):
    return (gate * jax.nn.sigmoid(gate) * up).astype(jnp.bfloat16)


def local(tokens, target, gate_panel, up_panel, down_panel, gate_list, up_list, down_list):
    n_hid, n_dp = lax.axis_size("hid"), lax.axis_size("dp")
    slab_blocks = FF // BLK // n_hid
    row_blocks = D // BLK // lax.axis_size("col")
    rows = tokens.shape[0]
    own = rows * n_hid

    def mine(block_list):
        share = block_list.shape[-1] // n_dp
        return lax.dynamic_slice_in_dim(block_list[0, 0], lax.axis_index("dp") * share, share)

    tables = (
        tile_table(gate_list[0, 0], row_blocks, slab_blocks, False),
        tile_table(up_list[0, 0], row_blocks, slab_blocks, False),
        tile_table(down_list[0, 0], row_blocks, slab_blocks, True),
        pick_codes(mine(gate_list), row_blocks, slab_blocks, False),
        pick_codes(mine(up_list), row_blocks, slab_blocks, False),
        pick_codes(mine(down_list), row_blocks, slab_blocks, True),
    )
    tables, gate_panel = lax.optimization_barrier((tables, gate_panel))
    gate_table, up_table, down_table, gate_codes, up_codes, down_codes = tables

    near, gate_table = lax.optimization_barrier((gather_near(tokens), gate_table))
    gate_w = densify(gate_panel[0, 0], gate_table, row_blocks, slab_blocks)
    inputs = jnp.concatenate(gather_far(near))

    gate_part = jnp.dot(inputs, gate_w, preferred_element_type=jnp.float32).astype(jnp.bfloat16)
    gate_other = swap_cores(gate_part)
    up_table, gate_part = lax.optimization_barrier((up_table, gate_part))
    up_w = densify(up_panel[0, 0], up_table, row_blocks, slab_blocks)
    up_part = jnp.dot(inputs, up_w, preferred_element_type=jnp.float32).astype(jnp.bfloat16)
    up_other = swap_cores(up_part)
    down_w = densify(down_panel[0, 0], down_table, slab_blocks, row_blocks)

    partials = (gate_part, gate_other, up_part, up_other)
    own_hidden, out_part = hidden_and_output(own, partials, down_w)
    sent = [out_part[k * rows : (k + 1) * rows] for k in range(n_hid)]
    moved = [shift(sent[k], "hid", k) for k in range(n_hid)]

    partials, own_hidden, out_part = lax.optimization_barrier((partials, own_hidden, out_part))
    gate = whole(*partials[:2])
    up = whole(*partials[2:])
    sigmoid_gate = jax.nn.sigmoid(gate)
    silu_gate = gate * sigmoid_gate
    hidden = jnp.concatenate([own_hidden, activation(gate[own:], up[own:])])
    gate_factor = up * sigmoid_gate * (1.0 + gate * (1.0 - sigmoid_gate))
    moved, silu_gate, hidden, gate_factor = lax.optimization_barrier(
        (moved, silu_gate, hidden, gate_factor)
    )

    output = f32(moved[0])
    for k in range(1, n_hid):
        output = output + f32(moved[k])
    own_slope = ((output - f32(target)) * SLOPE_SCALE).astype(jnp.bfloat16)
    slope = jnp.concatenate(gather_far(gather_near(own_slope)))
    back_part = back_product(slope, down_w)
    back_other = swap_cores(back_part)
    down_grad = gradient(hidden, (slope,), down_codes)
    gate_grad = gradient(inputs, (back_part, back_other, gate_factor), gate_codes)
    up_grad = gradient(inputs, (back_part, back_other, silu_gate), up_codes)
    return gate_grad[None, None], up_grad[None, None], down_grad[None, None]


def solution(mesh):
    return jax.shard_map(
        local,
        mesh=mesh,
        in_specs=(
            P(("groups", "hid", "dp"), "col"),
            P(("groups", "hid", "dp"), "col"),
            P(("groups", "hid"), "col", None, None),
            P(("groups", "hid"), "col", None, None),
            P(("groups", "hid"), "col", None, None),
            P(("groups", "hid"), "col", None),
            P(("groups", "hid"), "col", None),
            P(("groups", "hid"), "col", None),
        ),
        out_specs=(
            P(("groups", "hid"), "col", None, "dp"),
            P(("groups", "hid"), "col", None, "dp"),
            P(("groups", "hid"), "col", None, "dp"),
        ),
        check_vma=False,
    )
```

```python
import functools

import jax
import jax.numpy as jnp
from jax import lax
from jax.experimental import pallas as pl
from jax.experimental.pallas import tpu as pltpu
from jax.sharding import PartitionSpec as P

D = 4096
FF = 16384
BLK = 64
PAIR = 2 * BLK
SLOPE_SCALE = 0.0625
STAGE_VMEM = 15 * 2**20
PRODUCT_VMEM = 14 * 2**20
DEPTH_PART = 512
GRADIENT_VMEM = 44 * 2**20


def swap_halves(tile):
    return jnp.concatenate([tile[:, BLK:], tile[:, :BLK]], axis=1)


def join(left, right):
    return jnp.concatenate([left[:, :BLK], right[:, BLK:]], axis=1)


def lanes(t):
    return pl.ds(pl.multiple_of(t * PAIR, PAIR), PAIR)


def largest(options, total):
    return max(n for n in options if total % n == 0)


def stage_kernel(half_cap, chunks, panel, tiles, sems):
    share = half_cap // chunks
    copies = []
    for c in range(chunks):
        span = pl.ds(c * share * PAIR, share * PAIR)
        copies.append(pltpu.make_async_copy(panel.at[:, span], tiles.at[:, span], sems.at[c]))
        copies[c].start()
    tiles[:, 2 * half_cap * PAIR :] = jnp.zeros((BLK, PAIR), tiles.dtype)
    batch = largest((1, 2, 4, 5, 8, 10, 16, 20, 40), share)
    for c in range(chunks):
        copies[c].wait()

        def stage(b, carry):
            t = c * share + b * batch
            swapped = [swap_halves(tiles[:, lanes(t + u)]) for u in range(batch)]
            for u in range(batch):
                tiles[:, lanes(half_cap + t + u)] = swapped[u]
            return carry

        lax.fori_loop(0, share // batch, stage, 0)


def staged(panel):
    half_cap = panel.shape[1] // PAIR
    chunks = largest((1, 2, 4), half_cap)
    shape = (BLK, (2 * half_cap + 1) * PAIR)
    return pl.pallas_call(
        functools.partial(stage_kernel, half_cap, chunks),
        in_specs=[pl.BlockSpec(memory_space=pltpu.HBM)],
        out_specs=pl.BlockSpec(memory_space=pltpu.VMEM),
        out_shape=jax.ShapeDtypeStruct(shape, panel.dtype),
        scratch_shapes=[pltpu.SemaphoreType.DMA((chunks,))],
        compiler_params=pltpu.CompilerParams(vmem_limit_bytes=STAGE_VMEM),
        cost_estimate=pl.CostEstimate(flops=0, bytes_accessed=6 * panel.size, transcendentals=0),
        name="stage",
    )(pltpu.with_memory_space_constraint(panel, pltpu.HBM))


def place_kernel(rows_per_step, n_cols, table, tiles, out):
    step = pl.program_id(0)

    def row(i, carry):
        base = (step * rows_per_step + i) * n_cols
        for p in range(n_cols // 2):
            out[pl.ds(pl.multiple_of(i * BLK, BLK), BLK), p * PAIR : (p + 1) * PAIR] = join(
                tiles[:, lanes(table[base + 2 * p])], tiles[:, lanes(table[base + 2 * p + 1])]
            )
        return carry

    lax.fori_loop(0, rows_per_step, row, 0)


def place(tiles, table, n_rows, n_cols):
    rows_per_step = max(1, 128 // n_cols)
    return pl.pallas_call(
        functools.partial(place_kernel, rows_per_step, n_cols),
        grid_spec=pltpu.PrefetchScalarGridSpec(
            num_scalar_prefetch=1,
            grid=(n_rows // rows_per_step,),
            in_specs=[pl.BlockSpec(tiles.shape, lambda s, *_: (0, 0), pipeline_mode=pl.Buffered(1))],
            out_specs=pl.BlockSpec((rows_per_step * BLK, n_cols * BLK), lambda s, *_: (s, 0)),
        ),
        out_shape=jax.ShapeDtypeStruct((n_rows * BLK, n_cols * BLK), tiles.dtype),
        compiler_params=pltpu.CompilerParams(vmem_limit_bytes=STAGE_VMEM),
        cost_estimate=pl.CostEstimate(
            flops=0, bytes_accessed=2 * tiles.size + 4 * n_rows * n_cols * BLK * BLK, transcendentals=0
        ),
        name="place",
    )(table, tiles)


def gradient_kernel(n_steps, rows_per_step, n_cols, n_rhs, picks, lhs, *refs):
    terms, (out, tiles, rows) = refs[:n_rhs], refs[n_rhs : n_rhs + 3]
    step = pl.program_id(0)
    col_pairs = n_cols // 2
    width = 2
    rhs = terms[0]
    if n_rhs == 3:
        rhs = refs[n_rhs + 3]

        @pl.when(step == 0)
        def _():
            mine, theirs, factor = terms

            def scale(j, carry):
                span = pl.ds(pl.multiple_of(j * 2 * PAIR, 2 * PAIR), 2 * PAIR)
                rhs[:, span] = ((f32(mine[:, span]) + f32(theirs[:, span])) * factor[:, span]).astype(rhs.dtype)
                return carry

            lax.fori_loop(0, col_pairs // 2, scale, 0)

    rows[...] = lhs[...].T
    for c in range(0, col_pairs, width):
        part = jnp.dot(
            rows[...], rhs[:, c * PAIR : (c + width) * PAIR], preferred_element_type=jnp.float32
        ).astype(tiles.dtype)
        for i in range(rows_per_step):
            for p in range(width):
                tiles[(step * rows_per_step + i) * col_pairs + c + p] = part[
                    i * BLK : (i + 1) * BLK, p * PAIR : (p + 1) * PAIR
                ]

    @pl.when(step == n_steps - 1)
    def _():
        tiles[n_steps * rows_per_step * col_pairs] = jnp.zeros((BLK, PAIR), tiles.dtype)

        def pair(first, second):
            left, right = tiles[first >> 1], tiles[second >> 1]
            turn_left, turn_right = (first & 1) == 1, (second & 1) == 1
            turned = swap_halves(jnp.where(turn_left, jnp.where(turn_right, join(right, left), left), right))
            return join(jnp.where(turn_left, turned, left), jnp.where(turn_right, turned, right))

        pairs = out.shape[1] // PAIR
        batch = largest((1, 2, 5, 8, 10, 16), pairs)

        def pick(b, carry):
            k = b * batch
            kept = [pair(picks[2 * (k + u)], picks[2 * (k + u) + 1]) for u in range(batch)]
            for u in range(batch):
                out[:, lanes(k + u)] = kept[u]
            return carry

        lax.fori_loop(0, pairs // batch, pick, 0)


def gradient(lhs, terms, picks):
    n_rows, n_cols = lhs.shape[1] // BLK, terms[0].shape[1] // BLK
    rows_per_step = min(16, n_rows)
    n_steps = n_rows // rows_per_step
    scratch = [
        pltpu.VMEM((n_rows * n_cols // 2 + 1, BLK, PAIR), jnp.bfloat16),
        pltpu.VMEM((rows_per_step * BLK, lhs.shape[0]), jnp.bfloat16),
    ]
    if len(terms) == 3:
        scratch.append(pltpu.VMEM(terms[0].shape, jnp.bfloat16))
    return pl.pallas_call(
        functools.partial(gradient_kernel, n_steps, rows_per_step, n_cols, len(terms)),
        grid_spec=pltpu.PrefetchScalarGridSpec(
            num_scalar_prefetch=1,
            grid=(n_steps,),
            in_specs=[pl.BlockSpec((lhs.shape[0], rows_per_step * BLK), lambda s, *_: (0, s))]
            + [pl.BlockSpec(t.shape, lambda s, *_: (0, 0)) for t in terms],
            out_specs=pl.BlockSpec((BLK, picks.shape[0] * BLK), lambda s, *_: (0, 0)),
            scratch_shapes=scratch,
        ),
        out_shape=jax.ShapeDtypeStruct((BLK, picks.shape[0] * BLK), jnp.bfloat16),
        compiler_params=pltpu.CompilerParams(vmem_limit_bytes=GRADIENT_VMEM),
        cost_estimate=pl.CostEstimate(
            flops=2 * lhs.size * terms[0].shape[1],
            bytes_accessed=2 * lhs.size + 4 * len(terms) * terms[0].size + 2 * picks.shape[0] * BLK * BLK,
            transcendentals=0,
        ),
        name="gradient",
    )(picks, lhs, *terms)


def output_kernel(gate_mine, gate_theirs, up_mine, up_theirs, weights, hidden, out, total):
    step = pl.program_id(0)
    hidden[...] = activation(whole(gate_mine[...], gate_theirs[...]), whole(up_mine[...], up_theirs[...]))
    term = jnp.dot(hidden[...], weights[...], preferred_element_type=jnp.float32)

    @pl.when(step == 0)
    def _():
        total[...] = term

    @pl.when(step > 0)
    def _():
        total[...] += term

    @pl.when(step == pl.num_programs(0) - 1)
    def _():
        out[...] = total[...].astype(out.dtype)


def hidden_and_output(own, partials, weights):
    depth, width = weights.shape
    part = min(DEPTH_PART, depth)
    return pl.pallas_call(
        output_kernel,
        grid=(depth // part,),
        in_specs=[pl.BlockSpec((own, part), lambda s: (0, s))] * 4
        + [pl.BlockSpec((part, width), lambda s: (s, 0))],
        out_specs=[
            pl.BlockSpec((own, part), lambda s: (0, s)),
            pl.BlockSpec((own, width), lambda s: (0, 0)),
        ],
        out_shape=[
            jax.ShapeDtypeStruct((own, depth), jnp.bfloat16),
            jax.ShapeDtypeStruct((own, width), jnp.bfloat16),
        ],
        scratch_shapes=[pltpu.VMEM((own, width), jnp.float32)],
        compiler_params=pltpu.CompilerParams(vmem_limit_bytes=PRODUCT_VMEM),
        cost_estimate=pl.CostEstimate(
            flops=2 * own * depth * width,
            bytes_accessed=2 * (5 * own * depth + depth * width + own * width),
            transcendentals=own * depth,
        ),
        name="output",
    )(*partials, weights)


def forward_kernel(rows, weights, out):
    out[...] = jnp.dot(rows[...], weights[...], preferred_element_type=jnp.float32).astype(out.dtype)


def forward_product(rows, weights):
    depth, width = weights.shape
    part = min(512, width)
    return pl.pallas_call(
        forward_kernel,
        grid=(width // part,),
        in_specs=[
            pl.BlockSpec(rows.shape, lambda s: (0, 0)),
            pl.BlockSpec((depth, part), lambda s: (0, s)),
        ],
        out_specs=pl.BlockSpec((rows.shape[0], part), lambda s: (0, s)),
        out_shape=jax.ShapeDtypeStruct((rows.shape[0], width), jnp.bfloat16),
        compiler_params=pltpu.CompilerParams(vmem_limit_bytes=PRODUCT_VMEM),
        cost_estimate=pl.CostEstimate(
            flops=2 * rows.size * width,
            bytes_accessed=2 * (rows.size + weights.size + rows.shape[0] * width),
            transcendentals=0,
        ),
        name="forward",
    )(rows, weights)


def back_kernel(slope, weights, out):
    out[...] = lax.dot_general(
        slope[...], weights[...], (((1,), (1,)), ((), ())), preferred_element_type=jnp.float32
    ).astype(out.dtype)


def back_product(slope, weights):
    width, depth = weights.shape
    rows = slope.shape[0]
    part = min(512, width)
    return pl.pallas_call(
        back_kernel,
        grid=(width // part,),
        in_specs=[
            pl.BlockSpec((rows, depth), lambda s: (0, 0)),
            pl.BlockSpec((part, depth), lambda s: (s, 0)),
        ],
        out_specs=pl.BlockSpec((rows, part), lambda s: (0, s)),
        out_shape=jax.ShapeDtypeStruct((rows, width), jnp.bfloat16),
        compiler_params=pltpu.CompilerParams(vmem_limit_bytes=PRODUCT_VMEM),
        cost_estimate=pl.CostEstimate(
            flops=2 * rows * depth * width,
            bytes_accessed=2 * (rows * depth + depth * width + rows * width),
            transcendentals=0,
        ),
        name="back",
    )(slope, weights)


def tile_table(block_ids, row_blocks, slab_blocks, rows_are_hidden):
    cap = block_ids.shape[0]
    grid = row_blocks * slab_blocks
    slot = jnp.arange(1, cap + 1, dtype=jnp.int32)
    held = jnp.sum(
        jnp.where(block_ids[None, :] == jnp.arange(grid, dtype=jnp.int32)[:, None], slot[None, :], 0), axis=1
    )
    held = held.reshape(row_blocks, slab_blocks)
    if rows_are_hidden:
        held = held.T
    half = jnp.arange(held.shape[1], dtype=jnp.int32)[None, :] % 2
    index = held - 1
    tile = index // 2 + jnp.where(index % 2 != half, cap // 2, 0)
    return jnp.where(held > 0, tile, cap).reshape(-1)


def pick_codes(block_ids, row_blocks, slab_blocks, rows_are_hidden):
    grid = row_blocks * slab_blocks
    row, col = block_ids // slab_blocks, block_ids % slab_blocks
    cols = slab_blocks
    if rows_are_hidden:
        row, col, cols = col, row, row_blocks
    half = jnp.arange(block_ids.shape[0], dtype=jnp.int32) % 2
    code = 2 * (row * (cols // 2) + col // 2) + jnp.where(col % 2 != half, 1, 0)
    return jnp.where(block_ids < grid, code, grid)


def shift(values, axis, k):
    n = lax.axis_size(axis)
    return values if k == 0 else lax.ppermute(values, axis, [(i, i ^ k) for i in range(n)])


def gather_near(values):
    return [shift(values, "hid", k) for k in range(lax.axis_size("hid"))]


def gather_far(near):
    far = [shift(v, "dp", j) for j in range(1, lax.axis_size("dp")) for v in near]
    return near + far


def swap_cores(values):
    return lax.ppermute(values, "col", [(0, 1), (1, 0)])


def f32(values):
    return values.astype(jnp.float32)


def whole(mine, theirs):
    return f32(mine) + f32(theirs)


def activation(gate, up):
    return (gate * jax.nn.sigmoid(gate) * up).astype(jnp.bfloat16)


def local(tokens, target, gate_panel, up_panel, down_panel, gate_list, up_list, down_list):
    n_hid, n_dp = lax.axis_size("hid"), lax.axis_size("dp")
    slab_blocks = FF // BLK // n_hid
    row_blocks = D // BLK // lax.axis_size("col")
    rows = tokens.shape[0]
    own = rows * n_hid

    def mine(block_list):
        share = block_list.shape[-1] // n_dp
        return lax.dynamic_slice_in_dim(block_list[0, 0], lax.axis_index("dp") * share, share)

    tables = (
        tile_table(gate_list[0, 0], row_blocks, slab_blocks, False),
        tile_table(up_list[0, 0], row_blocks, slab_blocks, False),
        tile_table(down_list[0, 0], row_blocks, slab_blocks, True),
        pick_codes(mine(gate_list), row_blocks, slab_blocks, False),
        pick_codes(mine(up_list), row_blocks, slab_blocks, False),
        pick_codes(mine(down_list), row_blocks, slab_blocks, True),
    )
    tables, gate_panel = lax.optimization_barrier((tables, gate_panel))
    gate_table, up_table, down_table, gate_codes, up_codes, down_codes = tables

    near, gate_tiles = lax.optimization_barrier((gather_near(tokens), staged(gate_panel[0, 0])))
    inputs = jnp.concatenate(gather_far(near))
    gate_w = place(gate_tiles, gate_table, row_blocks, slab_blocks)
    up_panel, gate_w = lax.optimization_barrier((up_panel, gate_w))
    up_tiles = staged(up_panel[0, 0])
    inputs, up_tiles = lax.optimization_barrier((inputs, up_tiles))
    gate_part = forward_product(inputs, gate_w)
    gate_other = swap_cores(gate_part)
    up_table, gate_part = lax.optimization_barrier((up_table, gate_part))
    up_w = place(up_tiles, up_table, row_blocks, slab_blocks)
    up_part = jnp.dot(inputs, up_w, preferred_element_type=jnp.float32).astype(jnp.bfloat16)
    up_other = swap_cores(up_part)
    down_panel, up_part = lax.optimization_barrier((down_panel, up_part))
    down_w = place(staged(down_panel[0, 0]), down_table, slab_blocks, row_blocks)

    partials = (gate_part, gate_other, up_part, up_other)
    own_hidden, out_part = hidden_and_output(own, partials, down_w)
    sent = [out_part[k * rows : (k + 1) * rows] for k in range(n_hid)]
    moved = [shift(sent[k], "hid", k) for k in range(n_hid)]

    partials, own_hidden, out_part = lax.optimization_barrier((partials, own_hidden, out_part))
    gate = whole(*partials[:2])
    up = whole(*partials[2:])
    sigmoid_gate = jax.nn.sigmoid(gate)
    silu_gate = gate * sigmoid_gate
    hidden = jnp.concatenate([own_hidden, activation(gate[own:], up[own:])])
    gate_factor = up * sigmoid_gate * (1.0 + gate * (1.0 - sigmoid_gate))
    moved, silu_gate, hidden, gate_factor = lax.optimization_barrier(
        (moved, silu_gate, hidden, gate_factor)
    )

    output = f32(moved[0])
    for k in range(1, n_hid):
        output = output + f32(moved[k])
    own_slope = ((output - f32(target)) * SLOPE_SCALE).astype(jnp.bfloat16)
    slope = jnp.concatenate(gather_far(gather_near(own_slope)))
    back_part = back_product(slope, down_w)
    back_other = swap_cores(back_part)
    down_grad = gradient(hidden, (slope,), down_codes)
    gate_grad = gradient(inputs, (back_part, back_other, gate_factor), gate_codes)
    up_grad = gradient(inputs, (back_part, back_other, silu_gate), up_codes)
    return gate_grad[None, None], up_grad[None, None], down_grad[None, None]


def solution(mesh):
    return jax.shard_map(
        local,
        mesh=mesh,
        in_specs=(
            P(("groups", "hid", "dp"), "col"),
            P(("groups", "hid", "dp"), "col"),
            P(("groups", "hid"), "col", None, None),
            P(("groups", "hid"), "col", None, None),
            P(("groups", "hid"), "col", None, None),
            P(("groups", "hid"), "col", None),
            P(("groups", "hid"), "col", None),
            P(("groups", "hid"), "col", None),
        ),
        out_specs=(
            P(("groups", "hid"), "col", None, "dp"),
            P(("groups", "hid"), "col", None, "dp"),
            P(("groups", "hid"), "col", None, "dp"),
        ),
        check_vma=False,
    )
```

```python
import functools

import jax
import jax.numpy as jnp
from jax import lax
from jax.experimental import pallas as pl
from jax.experimental.pallas import tpu as pltpu
from jax.sharding import PartitionSpec as P

D = 4096
FF = 16384
BLK = 64
PAIR = 2 * BLK
SLOPE_SCALE = 0.0625
STAGE_VMEM = 15 * 2**20
PRODUCT_VMEM = 14 * 2**20
DEPTH_PART = 512
GRADIENT_VMEM = 44 * 2**20


def swap_halves(tile):
    return jnp.concatenate([tile[:, BLK:], tile[:, :BLK]], axis=1)


def join(left, right):
    return jnp.concatenate([left[:, :BLK], right[:, BLK:]], axis=1)


def lanes(t):
    return pl.ds(pl.multiple_of(t * PAIR, PAIR), PAIR)


def largest(options, total):
    return max(n for n in options if total % n == 0)


def stage_kernel(half_cap, chunks, panel, tiles, sems):
    share = half_cap // chunks
    copies = []
    for c in range(chunks):
        span = pl.ds(c * share * PAIR, share * PAIR)
        copies.append(pltpu.make_async_copy(panel.at[:, span], tiles.at[:, span], sems.at[c]))
        copies[c].start()
    tiles[:, 2 * half_cap * PAIR :] = jnp.zeros((BLK, PAIR), tiles.dtype)
    batch = largest((1, 2, 4, 5, 8, 10, 16, 20, 40), share)
    for c in range(chunks):
        copies[c].wait()

        def stage(b, carry):
            t = c * share + b * batch
            swapped = [swap_halves(tiles[:, lanes(t + u)]) for u in range(batch)]
            for u in range(batch):
                tiles[:, lanes(half_cap + t + u)] = swapped[u]
            return carry

        lax.fori_loop(0, share // batch, stage, 0)


def staged(panel):
    half_cap = panel.shape[1] // PAIR
    chunks = largest((1, 2, 4), half_cap)
    shape = (BLK, (2 * half_cap + 1) * PAIR)
    return pl.pallas_call(
        functools.partial(stage_kernel, half_cap, chunks),
        in_specs=[pl.BlockSpec(memory_space=pltpu.HBM)],
        out_specs=pl.BlockSpec(memory_space=pltpu.VMEM),
        out_shape=jax.ShapeDtypeStruct(shape, panel.dtype),
        scratch_shapes=[pltpu.SemaphoreType.DMA((chunks,))],
        compiler_params=pltpu.CompilerParams(vmem_limit_bytes=STAGE_VMEM),
        cost_estimate=pl.CostEstimate(flops=0, bytes_accessed=6 * panel.size, transcendentals=0),
        name="stage",
    )(pltpu.with_memory_space_constraint(panel, pltpu.HBM))


def place_kernel(rows_per_step, n_cols, table, tiles, out):
    step = pl.program_id(0)

    def row(i, carry):
        base = (step * rows_per_step + i) * n_cols
        for p in range(n_cols // 2):
            out[pl.ds(pl.multiple_of(i * BLK, BLK), BLK), p * PAIR : (p + 1) * PAIR] = join(
                tiles[:, lanes(table[base + 2 * p])], tiles[:, lanes(table[base + 2 * p + 1])]
            )
        return carry

    lax.fori_loop(0, rows_per_step, row, 0)


def place(tiles, table, n_rows, n_cols):
    rows_per_step = max(1, 128 // n_cols)
    return pl.pallas_call(
        functools.partial(place_kernel, rows_per_step, n_cols),
        grid_spec=pltpu.PrefetchScalarGridSpec(
            num_scalar_prefetch=1,
            grid=(n_rows // rows_per_step,),
            in_specs=[pl.BlockSpec(tiles.shape, lambda s, *_: (0, 0), pipeline_mode=pl.Buffered(1))],
            out_specs=pl.BlockSpec((rows_per_step * BLK, n_cols * BLK), lambda s, *_: (s, 0)),
        ),
        out_shape=jax.ShapeDtypeStruct((n_rows * BLK, n_cols * BLK), tiles.dtype),
        compiler_params=pltpu.CompilerParams(vmem_limit_bytes=STAGE_VMEM),
        cost_estimate=pl.CostEstimate(
            flops=0, bytes_accessed=2 * tiles.size + 4 * n_rows * n_cols * BLK * BLK, transcendentals=0
        ),
        name="place",
    )(table, tiles)


def gradient_kernel(n_steps, rows_per_step, n_cols, n_rhs, picks, lhs, *refs):
    terms, (out, tiles, rows) = refs[:n_rhs], refs[n_rhs : n_rhs + 3]
    step = pl.program_id(0)
    col_pairs = n_cols // 2
    width = 2
    rhs = terms[0]
    if n_rhs == 3:
        rhs = refs[n_rhs + 3]

        @pl.when(step == 0)
        def _():
            mine, theirs, factor = terms

            def scale(j, carry):
                span = pl.ds(pl.multiple_of(j * 2 * PAIR, 2 * PAIR), 2 * PAIR)
                rhs[:, span] = ((f32(mine[:, span]) + f32(theirs[:, span])) * factor[:, span]).astype(rhs.dtype)
                return carry

            lax.fori_loop(0, col_pairs // 2, scale, 0)

    rows[...] = lhs[...].T
    for c in range(0, col_pairs, width):
        part = jnp.dot(
            rows[...], rhs[:, c * PAIR : (c + width) * PAIR], preferred_element_type=jnp.float32
        ).astype(tiles.dtype)
        for i in range(rows_per_step):
            for p in range(width):
                tiles[(step * rows_per_step + i) * col_pairs + c + p] = part[
                    i * BLK : (i + 1) * BLK, p * PAIR : (p + 1) * PAIR
                ]

    @pl.when(step == n_steps - 1)
    def _():
        tiles[n_steps * rows_per_step * col_pairs] = jnp.zeros((BLK, PAIR), tiles.dtype)

        def pair(first, second):
            left, right = tiles[first >> 1], tiles[second >> 1]
            turn_left, turn_right = (first & 1) == 1, (second & 1) == 1
            turned = swap_halves(jnp.where(turn_left, jnp.where(turn_right, join(right, left), left), right))
            return join(jnp.where(turn_left, turned, left), jnp.where(turn_right, turned, right))

        pairs = out.shape[1] // PAIR
        batch = largest((1, 2, 5, 8, 10, 16), pairs)

        def pick(b, carry):
            k = b * batch
            kept = [pair(picks[2 * (k + u)], picks[2 * (k + u) + 1]) for u in range(batch)]
            for u in range(batch):
                out[:, lanes(k + u)] = kept[u]
            return carry

        lax.fori_loop(0, pairs // batch, pick, 0)


def gradient(lhs, terms, picks):
    n_rows, n_cols = lhs.shape[1] // BLK, terms[0].shape[1] // BLK
    rows_per_step = min(16, n_rows)
    n_steps = n_rows // rows_per_step
    scratch = [
        pltpu.VMEM((n_rows * n_cols // 2 + 1, BLK, PAIR), jnp.bfloat16),
        pltpu.VMEM((rows_per_step * BLK, lhs.shape[0]), jnp.bfloat16),
    ]
    if len(terms) == 3:
        scratch.append(pltpu.VMEM(terms[0].shape, jnp.bfloat16))
    return pl.pallas_call(
        functools.partial(gradient_kernel, n_steps, rows_per_step, n_cols, len(terms)),
        grid_spec=pltpu.PrefetchScalarGridSpec(
            num_scalar_prefetch=1,
            grid=(n_steps,),
            in_specs=[pl.BlockSpec((lhs.shape[0], rows_per_step * BLK), lambda s, *_: (0, s))]
            + [pl.BlockSpec(t.shape, lambda s, *_: (0, 0)) for t in terms],
            out_specs=pl.BlockSpec((BLK, picks.shape[0] * BLK), lambda s, *_: (0, 0)),
            scratch_shapes=scratch,
        ),
        out_shape=jax.ShapeDtypeStruct((BLK, picks.shape[0] * BLK), jnp.bfloat16),
        compiler_params=pltpu.CompilerParams(vmem_limit_bytes=GRADIENT_VMEM),
        cost_estimate=pl.CostEstimate(
            flops=2 * lhs.size * terms[0].shape[1],
            bytes_accessed=2 * lhs.size + 4 * len(terms) * terms[0].size + 2 * picks.shape[0] * BLK * BLK,
            transcendentals=0,
        ),
        name="gradient",
    )(picks, lhs, *terms)


def output_kernel(gate_mine, gate_theirs, up_mine, up_theirs, weights, hidden, out, total):
    step = pl.program_id(0)
    hidden[...] = activation(whole(gate_mine[...], gate_theirs[...]), whole(up_mine[...], up_theirs[...]))
    term = jnp.dot(hidden[...], weights[...], preferred_element_type=jnp.float32)

    @pl.when(step == 0)
    def _():
        total[...] = term

    @pl.when(step > 0)
    def _():
        total[...] += term

    @pl.when(step == pl.num_programs(0) - 1)
    def _():
        out[...] = total[...].astype(out.dtype)


def hidden_and_output(own, partials, weights):
    depth, width = weights.shape
    part = min(DEPTH_PART, depth)
    return pl.pallas_call(
        output_kernel,
        grid=(depth // part,),
        in_specs=[pl.BlockSpec((own, part), lambda s: (0, s))] * 4
        + [pl.BlockSpec((part, width), lambda s: (s, 0))],
        out_specs=[
            pl.BlockSpec((own, part), lambda s: (0, s)),
            pl.BlockSpec((own, width), lambda s: (0, 0)),
        ],
        out_shape=[
            jax.ShapeDtypeStruct((own, depth), jnp.bfloat16),
            jax.ShapeDtypeStruct((own, width), jnp.bfloat16),
        ],
        scratch_shapes=[pltpu.VMEM((own, width), jnp.float32)],
        compiler_params=pltpu.CompilerParams(vmem_limit_bytes=PRODUCT_VMEM),
        cost_estimate=pl.CostEstimate(
            flops=2 * own * depth * width,
            bytes_accessed=2 * (5 * own * depth + depth * width + own * width),
            transcendentals=own * depth,
        ),
        name="output",
    )(*partials, weights)


def forward_kernel(rows, weights, out):
    out[...] = jnp.dot(rows[...], weights[...], preferred_element_type=jnp.float32).astype(out.dtype)


def forward_product(rows, weights):
    depth, width = weights.shape
    part = min(1024, width)
    return pl.pallas_call(
        forward_kernel,
        grid=(width // part,),
        in_specs=[
            pl.BlockSpec(rows.shape, lambda s: (0, 0)),
            pl.BlockSpec((depth, part), lambda s: (0, s)),
        ],
        out_specs=pl.BlockSpec((rows.shape[0], part), lambda s: (0, s)),
        out_shape=jax.ShapeDtypeStruct((rows.shape[0], width), jnp.bfloat16),
        compiler_params=pltpu.CompilerParams(vmem_limit_bytes=PRODUCT_VMEM),
        cost_estimate=pl.CostEstimate(
            flops=2 * rows.size * width,
            bytes_accessed=2 * (rows.size + weights.size + rows.shape[0] * width),
            transcendentals=0,
        ),
        name="forward",
    )(rows, weights)


def back_kernel(slope, weights, out):
    out[...] = lax.dot_general(
        slope[...], weights[...], (((1,), (1,)), ((), ())), preferred_element_type=jnp.float32
    ).astype(out.dtype)


def back_product(slope, weights):
    width, depth = weights.shape
    rows = slope.shape[0]
    part = min(1024, width)
    return pl.pallas_call(
        back_kernel,
        grid=(width // part,),
        in_specs=[
            pl.BlockSpec((rows, depth), lambda s: (0, 0)),
            pl.BlockSpec((part, depth), lambda s: (s, 0)),
        ],
        out_specs=pl.BlockSpec((rows, part), lambda s: (0, s)),
        out_shape=jax.ShapeDtypeStruct((rows, width), jnp.bfloat16),
        compiler_params=pltpu.CompilerParams(vmem_limit_bytes=PRODUCT_VMEM),
        cost_estimate=pl.CostEstimate(
            flops=2 * rows * depth * width,
            bytes_accessed=2 * (rows * depth + depth * width + rows * width),
            transcendentals=0,
        ),
        name="back",
    )(slope, weights)


def tile_table(block_ids, row_blocks, slab_blocks, rows_are_hidden):
    cap = block_ids.shape[0]
    grid = row_blocks * slab_blocks
    slot = jnp.arange(1, cap + 1, dtype=jnp.int32)
    held = jnp.sum(
        jnp.where(block_ids[None, :] == jnp.arange(grid, dtype=jnp.int32)[:, None], slot[None, :], 0), axis=1
    )
    held = held.reshape(row_blocks, slab_blocks)
    if rows_are_hidden:
        held = held.T
    half = jnp.arange(held.shape[1], dtype=jnp.int32)[None, :] % 2
    index = held - 1
    tile = index // 2 + jnp.where(index % 2 != half, cap // 2, 0)
    return jnp.where(held > 0, tile, cap).reshape(-1)


def pick_codes(block_ids, row_blocks, slab_blocks, rows_are_hidden):
    grid = row_blocks * slab_blocks
    row, col = block_ids // slab_blocks, block_ids % slab_blocks
    cols = slab_blocks
    if rows_are_hidden:
        row, col, cols = col, row, row_blocks
    half = jnp.arange(block_ids.shape[0], dtype=jnp.int32) % 2
    code = 2 * (row * (cols // 2) + col // 2) + jnp.where(col % 2 != half, 1, 0)
    return jnp.where(block_ids < grid, code, grid)


def shift(values, axis, k):
    n = lax.axis_size(axis)
    return values if k == 0 else lax.ppermute(values, axis, [(i, i ^ k) for i in range(n)])


def gather_near(values):
    return [shift(values, "hid", k) for k in range(lax.axis_size("hid"))]


def gather_far(near):
    far = [shift(v, "dp", j) for j in range(1, lax.axis_size("dp")) for v in near]
    return near + far


def swap_cores(values):
    return lax.ppermute(values, "col", [(0, 1), (1, 0)])


def f32(values):
    return values.astype(jnp.float32)


def whole(mine, theirs):
    return f32(mine) + f32(theirs)


def activation(gate, up):
    return (gate * jax.nn.sigmoid(gate) * up).astype(jnp.bfloat16)


def local(tokens, target, gate_panel, up_panel, down_panel, gate_list, up_list, down_list):
    n_hid, n_dp = lax.axis_size("hid"), lax.axis_size("dp")
    slab_blocks = FF // BLK // n_hid
    row_blocks = D // BLK // lax.axis_size("col")
    rows = tokens.shape[0]
    own = rows * n_hid

    def mine(block_list):
        share = block_list.shape[-1] // n_dp
        return lax.dynamic_slice_in_dim(block_list[0, 0], lax.axis_index("dp") * share, share)

    tables = (
        tile_table(gate_list[0, 0], row_blocks, slab_blocks, False),
        tile_table(up_list[0, 0], row_blocks, slab_blocks, False),
        tile_table(down_list[0, 0], row_blocks, slab_blocks, True),
        pick_codes(mine(gate_list), row_blocks, slab_blocks, False),
        pick_codes(mine(up_list), row_blocks, slab_blocks, False),
        pick_codes(mine(down_list), row_blocks, slab_blocks, True),
    )
    tables, gate_panel = lax.optimization_barrier((tables, gate_panel))
    gate_table, up_table, down_table, gate_codes, up_codes, down_codes = tables

    near, gate_tiles = lax.optimization_barrier((gather_near(tokens), staged(gate_panel[0, 0])))
    inputs = jnp.concatenate(gather_far(near))
    gate_w = place(gate_tiles, gate_table, row_blocks, slab_blocks)
    up_panel, gate_w = lax.optimization_barrier((up_panel, gate_w))
    up_tiles = staged(up_panel[0, 0])
    inputs, up_tiles = lax.optimization_barrier((inputs, up_tiles))
    gate_part = forward_product(inputs, gate_w)
    gate_other = swap_cores(gate_part)
    up_table, gate_part = lax.optimization_barrier((up_table, gate_part))
    up_w = place(up_tiles, up_table, row_blocks, slab_blocks)
    up_part = jnp.dot(inputs, up_w, preferred_element_type=jnp.float32).astype(jnp.bfloat16)
    up_other = swap_cores(up_part)
    down_panel, up_part = lax.optimization_barrier((down_panel, up_part))
    down_w = place(staged(down_panel[0, 0]), down_table, slab_blocks, row_blocks)

    partials = (gate_part, gate_other, up_part, up_other)
    own_hidden, out_part = hidden_and_output(own, partials, down_w)
    sent = [out_part[k * rows : (k + 1) * rows] for k in range(n_hid)]
    moved = [shift(sent[k], "hid", k) for k in range(n_hid)]

    partials, own_hidden, out_part = lax.optimization_barrier((partials, own_hidden, out_part))
    gate = whole(*partials[:2])
    up = whole(*partials[2:])
    sigmoid_gate = jax.nn.sigmoid(gate)
    silu_gate = gate * sigmoid_gate
    hidden = jnp.concatenate([own_hidden, activation(gate[own:], up[own:])])
    gate_factor = up * sigmoid_gate * (1.0 + gate * (1.0 - sigmoid_gate))
    moved, silu_gate, hidden, gate_factor = lax.optimization_barrier(
        (moved, silu_gate, hidden, gate_factor)
    )

    output = f32(moved[0])
    for k in range(1, n_hid):
        output = output + f32(moved[k])
    own_slope = ((output - f32(target)) * SLOPE_SCALE).astype(jnp.bfloat16)
    slope = jnp.concatenate(gather_far(gather_near(own_slope)))
    back_part = back_product(slope, down_w)
    back_other = swap_cores(back_part)
    down_grad = gradient(hidden, (slope,), down_codes)
    gate_grad = gradient(inputs, (back_part, back_other, gate_factor), gate_codes)
    up_grad = gradient(inputs, (back_part, back_other, silu_gate), up_codes)
    return gate_grad[None, None], up_grad[None, None], down_grad[None, None]


def solution(mesh):
    return jax.shard_map(
        local,
        mesh=mesh,
        in_specs=(
            P(("groups", "hid", "dp"), "col"),
            P(("groups", "hid", "dp"), "col"),
            P(("groups", "hid"), "col", None, None),
            P(("groups", "hid"), "col", None, None),
            P(("groups", "hid"), "col", None, None),
            P(("groups", "hid"), "col", None),
            P(("groups", "hid"), "col", None),
            P(("groups", "hid"), "col", None),
        ),
        out_specs=(
            P(("groups", "hid"), "col", None, "dp"),
            P(("groups", "hid"), "col", None, "dp"),
            P(("groups", "hid"), "col", None, "dp"),
        ),
        check_vma=False,
    )
```

```python
import functools

import jax
import jax.numpy as jnp
from jax import lax
from jax.experimental import pallas as pl
from jax.experimental.pallas import tpu as pltpu
from jax.sharding import PartitionSpec as P

D = 4096
FF = 16384
BLK = 64
PAIR = 2 * BLK
SLOPE_SCALE = 0.0625
STAGE_VMEM = 15 * 2**20
PRODUCT_VMEM = 14 * 2**20
DEPTH_PART = 1024
GRADIENT_VMEM = 44 * 2**20


def swap_halves(tile):
    return jnp.concatenate([tile[:, BLK:], tile[:, :BLK]], axis=1)


def join(left, right):
    return jnp.concatenate([left[:, :BLK], right[:, BLK:]], axis=1)


def lanes(t):
    return pl.ds(pl.multiple_of(t * PAIR, PAIR), PAIR)


def largest(options, total):
    return max(n for n in options if total % n == 0)


def stage_kernel(half_cap, chunks, panel, tiles, sems):
    share = half_cap // chunks
    copies = []
    for c in range(chunks):
        span = pl.ds(c * share * PAIR, share * PAIR)
        copies.append(pltpu.make_async_copy(panel.at[:, span], tiles.at[:, span], sems.at[c]))
        copies[c].start()
    tiles[:, 2 * half_cap * PAIR :] = jnp.zeros((BLK, PAIR), tiles.dtype)
    batch = largest((1, 2, 4, 5, 8, 10, 16, 20, 40), share)
    for c in range(chunks):
        copies[c].wait()

        def stage(b, carry):
            t = c * share + b * batch
            swapped = [swap_halves(tiles[:, lanes(t + u)]) for u in range(batch)]
            for u in range(batch):
                tiles[:, lanes(half_cap + t + u)] = swapped[u]
            return carry

        lax.fori_loop(0, share // batch, stage, 0)


def staged(panel):
    half_cap = panel.shape[1] // PAIR
    chunks = largest((1, 2, 4), half_cap)
    shape = (BLK, (2 * half_cap + 1) * PAIR)
    return pl.pallas_call(
        functools.partial(stage_kernel, half_cap, chunks),
        in_specs=[pl.BlockSpec(memory_space=pltpu.HBM)],
        out_specs=pl.BlockSpec(memory_space=pltpu.VMEM),
        out_shape=jax.ShapeDtypeStruct(shape, panel.dtype),
        scratch_shapes=[pltpu.SemaphoreType.DMA((chunks,))],
        compiler_params=pltpu.CompilerParams(vmem_limit_bytes=STAGE_VMEM),
        cost_estimate=pl.CostEstimate(flops=0, bytes_accessed=6 * panel.size, transcendentals=0),
        name="stage",
    )(pltpu.with_memory_space_constraint(panel, pltpu.HBM))


def place_kernel(rows_per_step, n_cols, table, tiles, out):
    step = pl.program_id(0)

    def row(i, carry):
        base = (step * rows_per_step + i) * n_cols
        for p in range(n_cols // 2):
            out[pl.ds(pl.multiple_of(i * BLK, BLK), BLK), p * PAIR : (p + 1) * PAIR] = join(
                tiles[:, lanes(table[base + 2 * p])], tiles[:, lanes(table[base + 2 * p + 1])]
            )
        return carry

    lax.fori_loop(0, rows_per_step, row, 0)


def place(tiles, table, n_rows, n_cols):
    rows_per_step = max(1, 128 // n_cols)
    return pl.pallas_call(
        functools.partial(place_kernel, rows_per_step, n_cols),
        grid_spec=pltpu.PrefetchScalarGridSpec(
            num_scalar_prefetch=1,
            grid=(n_rows // rows_per_step,),
            in_specs=[pl.BlockSpec(tiles.shape, lambda s, *_: (0, 0), pipeline_mode=pl.Buffered(1))],
            out_specs=pl.BlockSpec((rows_per_step * BLK, n_cols * BLK), lambda s, *_: (s, 0)),
        ),
        out_shape=jax.ShapeDtypeStruct((n_rows * BLK, n_cols * BLK), tiles.dtype),
        compiler_params=pltpu.CompilerParams(vmem_limit_bytes=STAGE_VMEM),
        cost_estimate=pl.CostEstimate(
            flops=0, bytes_accessed=2 * tiles.size + 4 * n_rows * n_cols * BLK * BLK, transcendentals=0
        ),
        name="place",
    )(table, tiles)


def gradient_kernel(n_steps, rows_per_step, n_cols, n_rhs, picks, lhs, *refs):
    terms, (out, tiles, rows) = refs[:n_rhs], refs[n_rhs : n_rhs + 3]
    step = pl.program_id(0)
    col_pairs = n_cols // 2
    width = 2
    rhs = terms[0]
    if n_rhs == 3:
        rhs = refs[n_rhs + 3]

        @pl.when(step == 0)
        def _():
            mine, theirs, factor = terms

            def scale(j, carry):
                span = pl.ds(pl.multiple_of(j * 2 * PAIR, 2 * PAIR), 2 * PAIR)
                rhs[:, span] = ((f32(mine[:, span]) + f32(theirs[:, span])) * factor[:, span]).astype(rhs.dtype)
                return carry

            lax.fori_loop(0, col_pairs // 2, scale, 0)

    rows[...] = lhs[...].T
    for c in range(0, col_pairs, width):
        part = jnp.dot(
            rows[...], rhs[:, c * PAIR : (c + width) * PAIR], preferred_element_type=jnp.float32
        ).astype(tiles.dtype)
        for i in range(rows_per_step):
            for p in range(width):
                tiles[(step * rows_per_step + i) * col_pairs + c + p] = part[
                    i * BLK : (i + 1) * BLK, p * PAIR : (p + 1) * PAIR
                ]

    @pl.when(step == n_steps - 1)
    def _():
        tiles[n_steps * rows_per_step * col_pairs] = jnp.zeros((BLK, PAIR), tiles.dtype)

        def pair(first, second):
            left, right = tiles[first >> 1], tiles[second >> 1]
            turn_left, turn_right = (first & 1) == 1, (second & 1) == 1
            turned = swap_halves(jnp.where(turn_left, jnp.where(turn_right, join(right, left), left), right))
            return join(jnp.where(turn_left, turned, left), jnp.where(turn_right, turned, right))

        pairs = out.shape[1] // PAIR
        batch = largest((1, 2, 5, 8, 10, 16), pairs)

        def pick(b, carry):
            k = b * batch
            kept = [pair(picks[2 * (k + u)], picks[2 * (k + u) + 1]) for u in range(batch)]
            for u in range(batch):
                out[:, lanes(k + u)] = kept[u]
            return carry

        lax.fori_loop(0, pairs // batch, pick, 0)


def gradient(lhs, terms, picks):
    n_rows, n_cols = lhs.shape[1] // BLK, terms[0].shape[1] // BLK
    rows_per_step = min(32, n_rows)
    n_steps = n_rows // rows_per_step
    scratch = [
        pltpu.VMEM((n_rows * n_cols // 2 + 1, BLK, PAIR), jnp.bfloat16),
        pltpu.VMEM((rows_per_step * BLK, lhs.shape[0]), jnp.bfloat16),
    ]
    if len(terms) == 3:
        scratch.append(pltpu.VMEM(terms[0].shape, jnp.bfloat16))
    return pl.pallas_call(
        functools.partial(gradient_kernel, n_steps, rows_per_step, n_cols, len(terms)),
        grid_spec=pltpu.PrefetchScalarGridSpec(
            num_scalar_prefetch=1,
            grid=(n_steps,),
            in_specs=[pl.BlockSpec((lhs.shape[0], rows_per_step * BLK), lambda s, *_: (0, s))]
            + [pl.BlockSpec(t.shape, lambda s, *_: (0, 0)) for t in terms],
            out_specs=pl.BlockSpec((BLK, picks.shape[0] * BLK), lambda s, *_: (0, 0)),
            scratch_shapes=scratch,
        ),
        out_shape=jax.ShapeDtypeStruct((BLK, picks.shape[0] * BLK), jnp.bfloat16),
        compiler_params=pltpu.CompilerParams(vmem_limit_bytes=GRADIENT_VMEM),
        cost_estimate=pl.CostEstimate(
            flops=2 * lhs.size * terms[0].shape[1],
            bytes_accessed=2 * lhs.size + 4 * len(terms) * terms[0].size + 2 * picks.shape[0] * BLK * BLK,
            transcendentals=0,
        ),
        name="gradient",
    )(picks, lhs, *terms)


def output_kernel(gate_mine, gate_theirs, up_mine, up_theirs, weights, hidden, out, total):
    step = pl.program_id(0)
    hidden[...] = activation(whole(gate_mine[...], gate_theirs[...]), whole(up_mine[...], up_theirs[...]))
    term = jnp.dot(hidden[...], weights[...], preferred_element_type=jnp.float32)

    @pl.when(step == 0)
    def _():
        total[...] = term

    @pl.when(step > 0)
    def _():
        total[...] += term

    @pl.when(step == pl.num_programs(0) - 1)
    def _():
        out[...] = total[...].astype(out.dtype)


def hidden_and_output(own, partials, weights):
    depth, width = weights.shape
    part = min(DEPTH_PART, depth)
    return pl.pallas_call(
        output_kernel,
        grid=(depth // part,),
        in_specs=[pl.BlockSpec((own, part), lambda s: (0, s))] * 4
        + [pl.BlockSpec((part, width), lambda s: (s, 0))],
        out_specs=[
            pl.BlockSpec((own, part), lambda s: (0, s)),
            pl.BlockSpec((own, width), lambda s: (0, 0)),
        ],
        out_shape=[
            jax.ShapeDtypeStruct((own, depth), jnp.bfloat16),
            jax.ShapeDtypeStruct((own, width), jnp.bfloat16),
        ],
        scratch_shapes=[pltpu.VMEM((own, width), jnp.float32)],
        compiler_params=pltpu.CompilerParams(vmem_limit_bytes=PRODUCT_VMEM),
        cost_estimate=pl.CostEstimate(
            flops=2 * own * depth * width,
            bytes_accessed=2 * (5 * own * depth + depth * width + own * width),
            transcendentals=own * depth,
        ),
        name="output",
    )(*partials, weights)


def forward_kernel(rows, weights, out):
    out[...] = jnp.dot(rows[...], weights[...], preferred_element_type=jnp.float32).astype(out.dtype)


def forward_product(rows, weights):
    depth, width = weights.shape
    part = min(1024, width)
    return pl.pallas_call(
        forward_kernel,
        grid=(width // part,),
        in_specs=[
            pl.BlockSpec(rows.shape, lambda s: (0, 0)),
            pl.BlockSpec((depth, part), lambda s: (0, s)),
        ],
        out_specs=pl.BlockSpec((rows.shape[0], part), lambda s: (0, s)),
        out_shape=jax.ShapeDtypeStruct((rows.shape[0], width), jnp.bfloat16),
        compiler_params=pltpu.CompilerParams(vmem_limit_bytes=PRODUCT_VMEM),
        cost_estimate=pl.CostEstimate(
            flops=2 * rows.size * width,
            bytes_accessed=2 * (rows.size + weights.size + rows.shape[0] * width),
            transcendentals=0,
        ),
        name="forward",
    )(rows, weights)


def back_kernel(slope, weights, out):
    out[...] = lax.dot_general(
        slope[...], weights[...], (((1,), (1,)), ((), ())), preferred_element_type=jnp.float32
    ).astype(out.dtype)


def back_product(slope, weights):
    width, depth = weights.shape
    rows = slope.shape[0]
    part = min(1024, width)
    return pl.pallas_call(
        back_kernel,
        grid=(width // part,),
        in_specs=[
            pl.BlockSpec((rows, depth), lambda s: (0, 0)),
            pl.BlockSpec((part, depth), lambda s: (s, 0)),
        ],
        out_specs=pl.BlockSpec((rows, part), lambda s: (0, s)),
        out_shape=jax.ShapeDtypeStruct((rows, width), jnp.bfloat16),
        compiler_params=pltpu.CompilerParams(vmem_limit_bytes=PRODUCT_VMEM),
        cost_estimate=pl.CostEstimate(
            flops=2 * rows * depth * width,
            bytes_accessed=2 * (rows * depth + depth * width + rows * width),
            transcendentals=0,
        ),
        name="back",
    )(slope, weights)


def tile_table(block_ids, row_blocks, slab_blocks, rows_are_hidden):
    cap = block_ids.shape[0]
    grid = row_blocks * slab_blocks
    slot = jnp.arange(1, cap + 1, dtype=jnp.int32)
    held = jnp.sum(
        jnp.where(block_ids[None, :] == jnp.arange(grid, dtype=jnp.int32)[:, None], slot[None, :], 0), axis=1
    )
    held = held.reshape(row_blocks, slab_blocks)
    if rows_are_hidden:
        held = held.T
    half = jnp.arange(held.shape[1], dtype=jnp.int32)[None, :] % 2
    index = held - 1
    tile = index // 2 + jnp.where(index % 2 != half, cap // 2, 0)
    return jnp.where(held > 0, tile, cap).reshape(-1)


def pick_codes(block_ids, row_blocks, slab_blocks, rows_are_hidden):
    grid = row_blocks * slab_blocks
    row, col = block_ids // slab_blocks, block_ids % slab_blocks
    cols = slab_blocks
    if rows_are_hidden:
        row, col, cols = col, row, row_blocks
    half = jnp.arange(block_ids.shape[0], dtype=jnp.int32) % 2
    code = 2 * (row * (cols // 2) + col // 2) + jnp.where(col % 2 != half, 1, 0)
    return jnp.where(block_ids < grid, code, grid)


def shift(values, axis, k):
    n = lax.axis_size(axis)
    return values if k == 0 else lax.ppermute(values, axis, [(i, i ^ k) for i in range(n)])


def gather_near(values):
    return [shift(values, "hid", k) for k in range(lax.axis_size("hid"))]


def gather_far(near):
    far = [shift(v, "dp", j) for j in range(1, lax.axis_size("dp")) for v in near]
    return near + far


def swap_cores(values):
    return lax.ppermute(values, "col", [(0, 1), (1, 0)])


def f32(values):
    return values.astype(jnp.float32)


def whole(mine, theirs):
    return f32(mine) + f32(theirs)


def activation(gate, up):
    return (gate * jax.nn.sigmoid(gate) * up).astype(jnp.bfloat16)


def local(tokens, target, gate_panel, up_panel, down_panel, gate_list, up_list, down_list):
    n_hid, n_dp = lax.axis_size("hid"), lax.axis_size("dp")
    slab_blocks = FF // BLK // n_hid
    row_blocks = D // BLK // lax.axis_size("col")
    rows = tokens.shape[0]
    own = rows * n_hid

    def mine(block_list):
        share = block_list.shape[-1] // n_dp
        return lax.dynamic_slice_in_dim(block_list[0, 0], lax.axis_index("dp") * share, share)

    tables = (
        tile_table(gate_list[0, 0], row_blocks, slab_blocks, False),
        tile_table(up_list[0, 0], row_blocks, slab_blocks, False),
        tile_table(down_list[0, 0], row_blocks, slab_blocks, True),
        pick_codes(mine(gate_list), row_blocks, slab_blocks, False),
        pick_codes(mine(up_list), row_blocks, slab_blocks, False),
        pick_codes(mine(down_list), row_blocks, slab_blocks, True),
    )
    tables, gate_panel = lax.optimization_barrier((tables, gate_panel))
    gate_table, up_table, down_table, gate_codes, up_codes, down_codes = tables

    near, gate_tiles = lax.optimization_barrier((gather_near(tokens), staged(gate_panel[0, 0])))
    inputs = jnp.concatenate(gather_far(near))
    gate_w = place(gate_tiles, gate_table, row_blocks, slab_blocks)
    up_panel, gate_w = lax.optimization_barrier((up_panel, gate_w))
    up_tiles = staged(up_panel[0, 0])
    inputs, up_tiles = lax.optimization_barrier((inputs, up_tiles))
    gate_part = forward_product(inputs, gate_w)
    gate_other = swap_cores(gate_part)
    up_table, gate_part = lax.optimization_barrier((up_table, gate_part))
    up_w = place(up_tiles, up_table, row_blocks, slab_blocks)
    up_part = jnp.dot(inputs, up_w, preferred_element_type=jnp.float32).astype(jnp.bfloat16)
    up_other = swap_cores(up_part)
    down_panel, up_part = lax.optimization_barrier((down_panel, up_part))
    down_w = place(staged(down_panel[0, 0]), down_table, slab_blocks, row_blocks)

    partials = (gate_part, gate_other, up_part, up_other)
    own_hidden, out_part = hidden_and_output(own, partials, down_w)
    sent = [out_part[k * rows : (k + 1) * rows] for k in range(n_hid)]
    moved = [shift(sent[k], "hid", k) for k in range(n_hid)]

    partials, own_hidden, out_part = lax.optimization_barrier((partials, own_hidden, out_part))
    gate = whole(*partials[:2])
    up = whole(*partials[2:])
    sigmoid_gate = jax.nn.sigmoid(gate)
    silu_gate = gate * sigmoid_gate
    hidden = jnp.concatenate([own_hidden, activation(gate[own:], up[own:])])
    gate_factor = up * sigmoid_gate * (1.0 + gate * (1.0 - sigmoid_gate))
    moved, silu_gate, hidden, gate_factor = lax.optimization_barrier(
        (moved, silu_gate, hidden, gate_factor)
    )

    output = f32(moved[0])
    for k in range(1, n_hid):
        output = output + f32(moved[k])
    own_slope = ((output - f32(target)) * SLOPE_SCALE).astype(jnp.bfloat16)
    slope = jnp.concatenate(gather_far(gather_near(own_slope)))
    back_part = back_product(slope, down_w)
    back_other = swap_cores(back_part)
    down_grad = gradient(hidden, (slope,), down_codes)
    gate_grad = gradient(inputs, (back_part, back_other, gate_factor), gate_codes)
    up_grad = gradient(inputs, (back_part, back_other, silu_gate), up_codes)
    return gate_grad[None, None], up_grad[None, None], down_grad[None, None]


def solution(mesh):
    return jax.shard_map(
        local,
        mesh=mesh,
        in_specs=(
            P(("groups", "hid", "dp"), "col"),
            P(("groups", "hid", "dp"), "col"),
            P(("groups", "hid"), "col", None, None),
            P(("groups", "hid"), "col", None, None),
            P(("groups", "hid"), "col", None, None),
            P(("groups", "hid"), "col", None),
            P(("groups", "hid"), "col", None),
            P(("groups", "hid"), "col", None),
        ),
        out_specs=(
            P(("groups", "hid"), "col", None, "dp"),
            P(("groups", "hid"), "col", None, "dp"),
            P(("groups", "hid"), "col", None, "dp"),
        ),
        check_vma=False,
    )
```

```python
import functools

import jax
import jax.numpy as jnp
from jax import lax
from jax.experimental import pallas as pl
from jax.experimental.pallas import tpu as pltpu
from jax.sharding import PartitionSpec as P

D = 4096
FF = 16384
BLK = 64
PAIR = 2 * BLK
SLOPE_SCALE = 0.0625
STAGE_VMEM = 15 * 2**20
PRODUCT_VMEM = 14 * 2**20
DEPTH_PART = 1024
GRADIENT_VMEM = 44 * 2**20


def swap_halves(tile):
    return jnp.concatenate([tile[:, BLK:], tile[:, :BLK]], axis=1)


def join(left, right):
    return jnp.concatenate([left[:, :BLK], right[:, BLK:]], axis=1)


def lanes(t):
    return pl.ds(pl.multiple_of(t * PAIR, PAIR), PAIR)


def largest(options, total):
    return max(n for n in options if total % n == 0)


def stage_kernel(half_cap, chunks, panel, tiles, sems):
    share = half_cap // chunks
    copies = []
    for c in range(chunks):
        span = pl.ds(c * share * PAIR, share * PAIR)
        copies.append(pltpu.make_async_copy(panel.at[:, span], tiles.at[:, span], sems.at[c]))
        copies[c].start()
    tiles[:, 2 * half_cap * PAIR :] = jnp.zeros((BLK, PAIR), tiles.dtype)
    batch = largest((1, 2, 4, 5, 8, 10, 16, 20, 40), share)
    for c in range(chunks):
        copies[c].wait()

        def stage(b, carry):
            t = c * share + b * batch
            swapped = [swap_halves(tiles[:, lanes(t + u)]) for u in range(batch)]
            for u in range(batch):
                tiles[:, lanes(half_cap + t + u)] = swapped[u]
            return carry

        lax.fori_loop(0, share // batch, stage, 0)


def staged(panel):
    half_cap = panel.shape[1] // PAIR
    chunks = largest((1, 2, 4), half_cap)
    shape = (BLK, (2 * half_cap + 1) * PAIR)
    return pl.pallas_call(
        functools.partial(stage_kernel, half_cap, chunks),
        in_specs=[pl.BlockSpec(memory_space=pltpu.HBM)],
        out_specs=pl.BlockSpec(memory_space=pltpu.VMEM),
        out_shape=jax.ShapeDtypeStruct(shape, panel.dtype),
        scratch_shapes=[pltpu.SemaphoreType.DMA((chunks,))],
        compiler_params=pltpu.CompilerParams(vmem_limit_bytes=STAGE_VMEM),
        cost_estimate=pl.CostEstimate(flops=0, bytes_accessed=6 * panel.size, transcendentals=0),
        name="stage",
    )(pltpu.with_memory_space_constraint(panel, pltpu.HBM))


def place_kernel(rows_per_step, n_cols, table, tiles, out):
    step = pl.program_id(0)

    def row(i, carry):
        base = (step * rows_per_step + i) * n_cols
        for p in range(n_cols // 2):
            out[pl.ds(pl.multiple_of(i * BLK, BLK), BLK), p * PAIR : (p + 1) * PAIR] = join(
                tiles[:, lanes(table[base + 2 * p])], tiles[:, lanes(table[base + 2 * p + 1])]
            )
        return carry

    lax.fori_loop(0, rows_per_step, row, 0)


def place(tiles, table, n_rows, n_cols):
    rows_per_step = min(n_rows, max(1, 256 // n_cols))
    return pl.pallas_call(
        functools.partial(place_kernel, rows_per_step, n_cols),
        grid_spec=pltpu.PrefetchScalarGridSpec(
            num_scalar_prefetch=1,
            grid=(n_rows // rows_per_step,),
            in_specs=[pl.BlockSpec(tiles.shape, lambda s, *_: (0, 0), pipeline_mode=pl.Buffered(1))],
            out_specs=pl.BlockSpec((rows_per_step * BLK, n_cols * BLK), lambda s, *_: (s, 0)),
        ),
        out_shape=jax.ShapeDtypeStruct((n_rows * BLK, n_cols * BLK), tiles.dtype),
        compiler_params=pltpu.CompilerParams(vmem_limit_bytes=STAGE_VMEM),
        cost_estimate=pl.CostEstimate(
            flops=0, bytes_accessed=2 * tiles.size + 4 * n_rows * n_cols * BLK * BLK, transcendentals=0
        ),
        name="place",
    )(table, tiles)


def gradient_kernel(n_steps, rows_per_step, n_cols, n_rhs, picks, lhs, *refs):
    terms, (out, tiles, rows) = refs[:n_rhs], refs[n_rhs : n_rhs + 3]
    step = pl.program_id(0)
    col_pairs = n_cols // 2
    width = 2
    rhs = terms[0]
    if n_rhs == 3:
        rhs = refs[n_rhs + 3]

        @pl.when(step == 0)
        def _():
            mine, theirs, factor = terms

            def scale(j, carry):
                span = pl.ds(pl.multiple_of(j * 2 * PAIR, 2 * PAIR), 2 * PAIR)
                rhs[:, span] = ((f32(mine[:, span]) + f32(theirs[:, span])) * factor[:, span]).astype(rhs.dtype)
                return carry

            lax.fori_loop(0, col_pairs // 2, scale, 0)

    rows[...] = lhs[...].T
    for c in range(0, col_pairs, width):
        part = jnp.dot(
            rows[...], rhs[:, c * PAIR : (c + width) * PAIR], preferred_element_type=jnp.float32
        ).astype(tiles.dtype)
        for i in range(rows_per_step):
            for p in range(width):
                tiles[(step * rows_per_step + i) * col_pairs + c + p] = part[
                    i * BLK : (i + 1) * BLK, p * PAIR : (p + 1) * PAIR
                ]

    @pl.when(step == n_steps - 1)
    def _():
        tiles[n_steps * rows_per_step * col_pairs] = jnp.zeros((BLK, PAIR), tiles.dtype)

        def pair(first, second):
            left, right = tiles[first >> 1], tiles[second >> 1]
            turn_left, turn_right = (first & 1) == 1, (second & 1) == 1
            turned = swap_halves(jnp.where(turn_left, jnp.where(turn_right, join(right, left), left), right))
            return join(jnp.where(turn_left, turned, left), jnp.where(turn_right, turned, right))

        pairs = out.shape[1] // PAIR
        batch = largest((1, 2, 5, 8, 10, 16), pairs)

        def pick(b, carry):
            k = b * batch
            kept = [pair(picks[2 * (k + u)], picks[2 * (k + u) + 1]) for u in range(batch)]
            for u in range(batch):
                out[:, lanes(k + u)] = kept[u]
            return carry

        lax.fori_loop(0, pairs // batch, pick, 0)


def gradient(lhs, terms, picks):
    n_rows, n_cols = lhs.shape[1] // BLK, terms[0].shape[1] // BLK
    rows_per_step = min(32, n_rows)
    n_steps = n_rows // rows_per_step
    scratch = [
        pltpu.VMEM((n_rows * n_cols // 2 + 1, BLK, PAIR), jnp.bfloat16),
        pltpu.VMEM((rows_per_step * BLK, lhs.shape[0]), jnp.bfloat16),
    ]
    if len(terms) == 3:
        scratch.append(pltpu.VMEM(terms[0].shape, jnp.bfloat16))
    return pl.pallas_call(
        functools.partial(gradient_kernel, n_steps, rows_per_step, n_cols, len(terms)),
        grid_spec=pltpu.PrefetchScalarGridSpec(
            num_scalar_prefetch=1,
            grid=(n_steps,),
            in_specs=[pl.BlockSpec((lhs.shape[0], rows_per_step * BLK), lambda s, *_: (0, s))]
            + [pl.BlockSpec(t.shape, lambda s, *_: (0, 0)) for t in terms],
            out_specs=pl.BlockSpec((BLK, picks.shape[0] * BLK), lambda s, *_: (0, 0)),
            scratch_shapes=scratch,
        ),
        out_shape=jax.ShapeDtypeStruct((BLK, picks.shape[0] * BLK), jnp.bfloat16),
        compiler_params=pltpu.CompilerParams(vmem_limit_bytes=GRADIENT_VMEM),
        cost_estimate=pl.CostEstimate(
            flops=2 * lhs.size * terms[0].shape[1],
            bytes_accessed=2 * lhs.size + 4 * len(terms) * terms[0].size + 2 * picks.shape[0] * BLK * BLK,
            transcendentals=0,
        ),
        name="gradient",
    )(picks, lhs, *terms)


def output_kernel(gate_mine, gate_theirs, up_mine, up_theirs, weights, hidden, out, total):
    step = pl.program_id(0)
    hidden[...] = activation(whole(gate_mine[...], gate_theirs[...]), whole(up_mine[...], up_theirs[...]))
    term = jnp.dot(hidden[...], weights[...], preferred_element_type=jnp.float32)

    @pl.when(step == 0)
    def _():
        total[...] = term

    @pl.when(step > 0)
    def _():
        total[...] += term

    @pl.when(step == pl.num_programs(0) - 1)
    def _():
        out[...] = total[...].astype(out.dtype)


def hidden_and_output(own, partials, weights):
    depth, width = weights.shape
    part = min(DEPTH_PART, depth)
    return pl.pallas_call(
        output_kernel,
        grid=(depth // part,),
        in_specs=[pl.BlockSpec((own, part), lambda s: (0, s))] * 4
        + [pl.BlockSpec((part, width), lambda s: (s, 0))],
        out_specs=[
            pl.BlockSpec((own, part), lambda s: (0, s)),
            pl.BlockSpec((own, width), lambda s: (0, 0)),
        ],
        out_shape=[
            jax.ShapeDtypeStruct((own, depth), jnp.bfloat16),
            jax.ShapeDtypeStruct((own, width), jnp.bfloat16),
        ],
        scratch_shapes=[pltpu.VMEM((own, width), jnp.float32)],
        compiler_params=pltpu.CompilerParams(vmem_limit_bytes=PRODUCT_VMEM),
        cost_estimate=pl.CostEstimate(
            flops=2 * own * depth * width,
            bytes_accessed=2 * (5 * own * depth + depth * width + own * width),
            transcendentals=own * depth,
        ),
        name="output",
    )(*partials, weights)


def forward_kernel(rows, weights, out):
    out[...] = jnp.dot(rows[...], weights[...], preferred_element_type=jnp.float32).astype(out.dtype)


def forward_product(rows, weights):
    depth, width = weights.shape
    part = min(1024, width)
    return pl.pallas_call(
        forward_kernel,
        grid=(width // part,),
        in_specs=[
            pl.BlockSpec(rows.shape, lambda s: (0, 0)),
            pl.BlockSpec((depth, part), lambda s: (0, s)),
        ],
        out_specs=pl.BlockSpec((rows.shape[0], part), lambda s: (0, s)),
        out_shape=jax.ShapeDtypeStruct((rows.shape[0], width), jnp.bfloat16),
        compiler_params=pltpu.CompilerParams(vmem_limit_bytes=PRODUCT_VMEM),
        cost_estimate=pl.CostEstimate(
            flops=2 * rows.size * width,
            bytes_accessed=2 * (rows.size + weights.size + rows.shape[0] * width),
            transcendentals=0,
        ),
        name="forward",
    )(rows, weights)


def back_kernel(slope, weights, out):
    out[...] = lax.dot_general(
        slope[...], weights[...], (((1,), (1,)), ((), ())), preferred_element_type=jnp.float32
    ).astype(out.dtype)


def back_product(slope, weights):
    width, depth = weights.shape
    rows = slope.shape[0]
    part = min(1024, width)
    return pl.pallas_call(
        back_kernel,
        grid=(width // part,),
        in_specs=[
            pl.BlockSpec((rows, depth), lambda s: (0, 0)),
            pl.BlockSpec((part, depth), lambda s: (s, 0)),
        ],
        out_specs=pl.BlockSpec((rows, part), lambda s: (0, s)),
        out_shape=jax.ShapeDtypeStruct((rows, width), jnp.bfloat16),
        compiler_params=pltpu.CompilerParams(vmem_limit_bytes=PRODUCT_VMEM),
        cost_estimate=pl.CostEstimate(
            flops=2 * rows * depth * width,
            bytes_accessed=2 * (rows * depth + depth * width + rows * width),
            transcendentals=0,
        ),
        name="back",
    )(slope, weights)


def tile_table(block_ids, row_blocks, slab_blocks, rows_are_hidden):
    cap = block_ids.shape[0]
    grid = row_blocks * slab_blocks
    slot = jnp.arange(1, cap + 1, dtype=jnp.int32)
    held = jnp.sum(
        jnp.where(block_ids[None, :] == jnp.arange(grid, dtype=jnp.int32)[:, None], slot[None, :], 0), axis=1
    )
    held = held.reshape(row_blocks, slab_blocks)
    if rows_are_hidden:
        held = held.T
    half = jnp.arange(held.shape[1], dtype=jnp.int32)[None, :] % 2
    index = held - 1
    tile = index // 2 + jnp.where(index % 2 != half, cap // 2, 0)
    return jnp.where(held > 0, tile, cap).reshape(-1)


def pick_codes(block_ids, row_blocks, slab_blocks, rows_are_hidden):
    grid = row_blocks * slab_blocks
    row, col = block_ids // slab_blocks, block_ids % slab_blocks
    cols = slab_blocks
    if rows_are_hidden:
        row, col, cols = col, row, row_blocks
    half = jnp.arange(block_ids.shape[0], dtype=jnp.int32) % 2
    code = 2 * (row * (cols // 2) + col // 2) + jnp.where(col % 2 != half, 1, 0)
    return jnp.where(block_ids < grid, code, grid)


def shift(values, axis, k):
    n = lax.axis_size(axis)
    return values if k == 0 else lax.ppermute(values, axis, [(i, i ^ k) for i in range(n)])


def gather_near(values):
    return [shift(values, "hid", k) for k in range(lax.axis_size("hid"))]


def gather_far(near):
    far = [shift(v, "dp", j) for j in range(1, lax.axis_size("dp")) for v in near]
    return near + far


def swap_cores(values):
    return lax.ppermute(values, "col", [(0, 1), (1, 0)])


def f32(values):
    return values.astype(jnp.float32)


def whole(mine, theirs):
    return f32(mine) + f32(theirs)


def activation(gate, up):
    return (gate * jax.nn.sigmoid(gate) * up).astype(jnp.bfloat16)


def local(tokens, target, gate_panel, up_panel, down_panel, gate_list, up_list, down_list):
    n_hid, n_dp = lax.axis_size("hid"), lax.axis_size("dp")
    slab_blocks = FF // BLK // n_hid
    row_blocks = D // BLK // lax.axis_size("col")
    rows = tokens.shape[0]
    own = rows * n_hid

    def mine(block_list):
        share = block_list.shape[-1] // n_dp
        return lax.dynamic_slice_in_dim(block_list[0, 0], lax.axis_index("dp") * share, share)

    tables = (
        tile_table(gate_list[0, 0], row_blocks, slab_blocks, False),
        tile_table(up_list[0, 0], row_blocks, slab_blocks, False),
        tile_table(down_list[0, 0], row_blocks, slab_blocks, True),
        pick_codes(mine(gate_list), row_blocks, slab_blocks, False),
        pick_codes(mine(up_list), row_blocks, slab_blocks, False),
        pick_codes(mine(down_list), row_blocks, slab_blocks, True),
    )
    tables, gate_panel = lax.optimization_barrier((tables, gate_panel))
    gate_table, up_table, down_table, gate_codes, up_codes, down_codes = tables

    near, gate_tiles = lax.optimization_barrier((gather_near(tokens), staged(gate_panel[0, 0])))
    inputs = jnp.concatenate(gather_far(near))
    gate_w = place(gate_tiles, gate_table, row_blocks, slab_blocks)
    up_panel, gate_w = lax.optimization_barrier((up_panel, gate_w))
    up_tiles = staged(up_panel[0, 0])
    inputs, up_tiles = lax.optimization_barrier((inputs, up_tiles))
    gate_part = forward_product(inputs, gate_w)
    gate_other = swap_cores(gate_part)
    up_table, gate_part = lax.optimization_barrier((up_table, gate_part))
    up_w = place(up_tiles, up_table, row_blocks, slab_blocks)
    up_part = jnp.dot(inputs, up_w, preferred_element_type=jnp.float32).astype(jnp.bfloat16)
    up_other = swap_cores(up_part)
    down_panel, up_part = lax.optimization_barrier((down_panel, up_part))
    down_w = place(staged(down_panel[0, 0]), down_table, slab_blocks, row_blocks)

    partials = (gate_part, gate_other, up_part, up_other)
    own_hidden, out_part = hidden_and_output(own, partials, down_w)
    sent = [out_part[k * rows : (k + 1) * rows] for k in range(n_hid)]
    moved = [shift(sent[k], "hid", k) for k in range(n_hid)]

    partials, own_hidden, out_part = lax.optimization_barrier((partials, own_hidden, out_part))
    gate = whole(*partials[:2])
    up = whole(*partials[2:])
    sigmoid_gate = jax.nn.sigmoid(gate)
    silu_gate = gate * sigmoid_gate
    hidden = jnp.concatenate([own_hidden, activation(gate[own:], up[own:])])
    gate_factor = up * sigmoid_gate * (1.0 + gate * (1.0 - sigmoid_gate))
    moved, silu_gate, hidden, gate_factor = lax.optimization_barrier(
        (moved, silu_gate, hidden, gate_factor)
    )

    output = f32(moved[0])
    for k in range(1, n_hid):
        output = output + f32(moved[k])
    own_slope = ((output - f32(target)) * SLOPE_SCALE).astype(jnp.bfloat16)
    slope = jnp.concatenate(gather_far(gather_near(own_slope)))
    back_part = back_product(slope, down_w)
    back_other = swap_cores(back_part)
    down_grad = gradient(hidden, (slope,), down_codes)
    gate_grad = gradient(inputs, (back_part, back_other, gate_factor), gate_codes)
    up_grad = gradient(inputs, (back_part, back_other, silu_gate), up_codes)
    return gate_grad[None, None], up_grad[None, None], down_grad[None, None]


def solution(mesh):
    return jax.shard_map(
        local,
        mesh=mesh,
        in_specs=(
            P(("groups", "hid", "dp"), "col"),
            P(("groups", "hid", "dp"), "col"),
            P(("groups", "hid"), "col", None, None),
            P(("groups", "hid"), "col", None, None),
            P(("groups", "hid"), "col", None, None),
            P(("groups", "hid"), "col", None),
            P(("groups", "hid"), "col", None),
            P(("groups", "hid"), "col", None),
        ),
        out_specs=(
            P(("groups", "hid"), "col", None, "dp"),
            P(("groups", "hid"), "col", None, "dp"),
            P(("groups", "hid"), "col", None, "dp"),
        ),
        check_vma=False,
    )
```
